512 devices in a mesh: rows: 128 (over z, y, core), rep: 4 (over x).
Axes of the slice: x: 4, y: 4, z: 16, core: 2. Of those that a mesh axis runs over, the one named last changes fastest.
Arguments:
- embeddings: bfloat16 [65536, 1024], P(('rows', 'rep')), may hold values from -6 to 6
- parent_id: int32 [65536], P(('rows', 'rep')), may hold values from 0 to 1023
- send_list: int32 [512, 128, 2], P(('rows', 'rep')), may hold values from 0 to 127, as said below
- send_count: int32 [512, 128], P(('rows', 'rep')), may hold values from 0 to 2, as said below
- child_count: int32 [1024], P('rows'), may hold values from 64 to 128, as said below
- centroids: bfloat16 [1024, 128, 1024], P('rows'), may hold values from -24 to 24
Outputs:
- updated_centroids: float32 [1024, 128, 1024], P('rows', 'rep')
- row_energy: float32 [65536], P(('rows', 'rep'))
The draws below stay inside these ranges and needn't reach their ends.
Inputs may be any that keep to these rules, and one draw needn't show every extreme that they name: For device d and owner o, the first send_count[d, o] entries of send_list[d, o] name distinct local rows whose parent_id // 8 == o; every local row of d is named exactly once over all owners; entries past the count are 0. `send_count`: each device's counts sum to 128; one owner, the same for every device, gets exactly 2 rows from every device. `child_count`: some parent has 128 live children.
All inputs are finite; a program needn't handle non-finite values.
Results may differ from the reference program's by a relative error of at most 0.0038.
Values may be sent and summed in bfloat16 or wider, within the bound.
A program may use at most 64 MiB of HBM per device.

```python
import jax
import jax.numpy as jnp
from jax import lax

D = 1024
K = 128
PAR_DEV = 8
ROW_DEV = 128
ITERS = 2
CAP = 2
ROWS = 65536
PARENTS = 1024
N_ROWS = 128
N_REP = 4


def routing(key):
    senders = N_ROWS * N_REP
    position_overall_sum = N_ROWS * CAP
    heaviest_holder = jax.random.randint(jax.random.fold_in(key, 101), (), 0, N_ROWS)
    raw_affinities = jax.random.randint(jax.random.fold_in(key, 102), (senders, position_overall_sum), 0, 2 ** 18)
    position_numbers = jnp.arange(position_overall_sum, dtype=jnp.int32)
    holder_table = position_numbers // CAP
    affinity_offset = jnp.where(holder_table == heaviest_holder, 2 ** 30, 0).astype(jnp.int32)
    affinity_matrix = raw_affinities * position_overall_sum + position_numbers[None, :] + affinity_offset[None, :]
    unused_values, chosen_idx = lax.top_k(affinity_matrix, ROW_DEV)
    sender_ids = jnp.arange(senders, dtype=jnp.int32)[:, None]
    chosen = jnp.zeros((senders, position_overall_sum), jnp.int32).at[sender_ids, chosen_idx].set(1)
    rank = jnp.clip(jnp.cumsum(chosen, axis=1) - 1, 0, ROW_DEV - 1)
    shuffles = jax.vmap(lambda sub_key: jax.random.permutation(sub_key, ROW_DEV))(jax.random.split(jax.random.fold_in(key, 103), senders))
    row_of_slot = jnp.take_along_axis(shuffles.astype(jnp.int32), rank, axis=1)
    chosen_cube = chosen.reshape(senders, N_ROWS, CAP)
    position = jnp.cumsum(chosen_cube, axis=2) - 1
    counting = jnp.sum(chosen_cube, axis=2).astype(jnp.int32)
    target_pos = jnp.where(chosen_cube == 1, position, CAP)
    owner_ids = jnp.arange(N_ROWS, dtype=jnp.int32)[None, :, None]
    listing = jnp.zeros((senders, N_ROWS, CAP), jnp.int32).at[sender_ids[:, :, None], owner_ids, target_pos].set(row_of_slot.reshape(senders, N_ROWS, CAP), mode='drop')
    sub_pick = jax.random.randint(jax.random.fold_in(key, 104), (senders, position_overall_sum), 0, PAR_DEV)
    parent_slot = holder_table[None, :] * PAR_DEV + sub_pick
    target_row = jnp.where(chosen == 1, row_of_slot, ROW_DEV)
    parents = jnp.zeros((senders, ROW_DEV), jnp.int32).at[sender_ids, target_row].set(parent_slot, mode='drop')
    return (listing, counting, parents.reshape(-1))


def draw_send_list(key, part):
    return routing(key)[0]


def draw_send_count(key, part):
    return routing(key)[1]


def draw_parent_id(key, part):
    return routing(key)[2]


def draw_child_count(key, part):
    key = jax.random.fold_in(key, 7)
    counts = jax.random.randint(jax.random.fold_in(key, 1), (PARENTS,), K // 2, K + 1)
    first = jax.random.randint(jax.random.fold_in(key, 2), (), 0, PARENTS)
    counts = counts.at[first].set(K)
    counts = counts.at[(first + 1) % PARENTS].set(K // 2)
    return counts.astype(jnp.int32)


def draw_centroids(key, part):
    key = jax.random.fold_in(key, 11)
    values = jnp.clip(jax.random.normal(jax.random.fold_in(key, 1), (PARENTS, K, D), jnp.float32), -6.0, 6.0)
    return values.astype(jnp.bfloat16)


def level_of(own_key, shape, cuts, low, high):
    loudness = 1.0
    for dim, parts in cuts:
        steps = jax.random.uniform(jax.random.fold_in(jax.random.fold_in(own_key, 6), dim), (parts,), jnp.float32, low / len(cuts), high / len(cuts))
        loudness = loudness * jnp.repeat(jnp.exp(steps), shape[dim] // parts).reshape((-1,) + (1,) * (len(shape) - 1 - dim))
    return loudness


def normal_values(stream_key, shape, spread, bound, cuts=(), held_as=jnp.bfloat16):
    gain = level_of(stream_key, shape, cuts, -0.22, 0.18) if cuts else 1.0
    result = jax.random.normal(stream_key, shape, jnp.float32) * spread * gain
    return jnp.minimum(jnp.maximum(result, -bound), bound).astype(held_as)


def setup_inputs(seed: int = 0) -> dict:
    keys = jax.random.split(jax.random.key(seed), 7)
    return {
        "embeddings": normal_values(keys[0], (ROWS, D), 1.0, 6.0, ((0, 512),)),
        "parent_id": draw_parent_id(jax.random.fold_in(keys[6], 71), 0),
        "send_list": draw_send_list(jax.random.fold_in(keys[6], 71), 0),
        "send_count": draw_send_count(jax.random.fold_in(keys[6], 71), 0),
        "child_count": draw_child_count(jax.random.fold_in(keys[6], 71), 0),
        "centroids": draw_centroids(jax.random.fold_in(keys[6], 71), 0),
    }


inverse_temp = 1.0 / 32.0
prior_weight = 1.0


def block_terms(row_block, sub_rows, live_rows, child_panel, child_count):
    par_dev, kids, width = child_panel.shape
    flat_kids = child_panel.reshape(par_dev * kids, width)
    raw_affinities = jnp.dot(row_block, flat_kids.T, preferred_element_type=jnp.float32)
    kid_norms = jnp.sum(jnp.square(flat_kids.astype(jnp.float32)), axis=1)
    column = jnp.arange(par_dev * kids, dtype=jnp.int32)
    column_parent = column // kids
    column_open = (column % kids) < jnp.repeat(child_count, kids)
    allowed = (column_parent[None, :] == sub_rows[:, None]) & column_open[None, :]
    logits = jnp.where(allowed, (2.0 * raw_affinities - kid_norms[None, :]) * inverse_temp, -jnp.inf)
    row_top = jnp.max(logits, axis=1)
    exp_terms = jnp.where(allowed, jnp.exp(logits - row_top[:, None]), 0.0)
    exp_total = jnp.sum(exp_terms, axis=1)
    energy = row_top + jnp.log(exp_total)
    weights_full = exp_terms / exp_total[:, None] * live_rows[:, None]
    weights_half = weights_full.astype(jnp.bfloat16)
    sum_rows = jnp.dot(weights_half.T, row_block, preferred_element_type=jnp.float32)
    return sum_rows, jnp.sum(weights_full, axis=0), energy


def reference(embeddings, parent_id, send_list, send_count, child_count, centroids):
    senders = N_ROWS * N_REP
    slot_width = send_list.shape[2]
    filled = jnp.arange(slot_width, dtype=jnp.int32)[None, None, :] < send_count[:, :, None]
    row_base = (jnp.arange(senders, dtype=jnp.int32) * ROW_DEV)[:, None, None]
    global_rows = row_base + send_list
    sub_all = parent_id[global_rows] % PAR_DEV

    def one_pass(child_panels):
        def owner_pass(owner_pos):
            child_panel = lax.dynamic_slice_in_dim(child_panels, owner_pos * PAR_DEV, PAR_DEV, 0)
            counts = lax.dynamic_slice_in_dim(child_count, owner_pos * PAR_DEV, PAR_DEV, 0)
            total_sums = jnp.zeros((PAR_DEV * K, D), jnp.float32)
            total_weights = jnp.zeros((PAR_DEV * K,), jnp.float32)
            energies = []
            for rep_pos in range(N_REP):
                senders_here = jnp.arange(N_ROWS, dtype=jnp.int32) * N_REP + rep_pos
                slot_rows = global_rows[senders_here, owner_pos].reshape(-1)
                sub_rows = sub_all[senders_here, owner_pos].reshape(-1)
                live_rows = filled[senders_here, owner_pos].reshape(-1).astype(jnp.float32)
                row_block = embeddings[slot_rows]
                sum_rows, weight_rows, energy = block_terms(row_block, sub_rows, live_rows, child_panel, counts)
                total_sums = total_sums + lax.optimization_barrier(sum_rows.astype(jnp.bfloat16)).astype(jnp.float32)
                total_weights = total_weights + weight_rows
                energies.append(energy)
            return total_sums, total_weights, jnp.stack(energies)

        return lax.map(owner_pass, jnp.arange(N_ROWS, dtype=jnp.int32))

    child_panels = centroids
    for iteration in range(ITERS):
        old_kids = child_panels.astype(jnp.float32)
        sum_all, weight_all, energy_all = one_pass(child_panels)
        sum_all = sum_all.reshape(PARENTS, K, D)
        weight_all = weight_all.reshape(PARENTS, K)
        new_kids = (sum_all + prior_weight * old_kids) / (weight_all[:, :, None] + prior_weight)
        child_panels = new_kids.astype(jnp.bfloat16)

    order_rows = global_rows.reshape(N_ROWS, N_REP, N_ROWS, slot_width).transpose(2, 1, 0, 3).reshape(-1)
    order_live = filled.reshape(N_ROWS, N_REP, N_ROWS, slot_width).transpose(2, 1, 0, 3).reshape(-1)
    values = jnp.where(order_live, energy_all.reshape(-1), 0.0)
    row_energy = jnp.zeros((ROWS,), jnp.float32).at[order_rows].add(values)
    return new_kids, row_energy
```

```python
import functools

import jax
import jax.numpy as jnp
from jax import lax
from jax.experimental import pallas as pl
from jax.experimental.pallas import tpu as pltpu
from jax.sharding import PartitionSpec as P

MESH = pl.DeviceIdType.MESH
F32 = jnp.float32
BF16 = jnp.bfloat16

NZ, NG, NQ = 16, 8, 4
NR = NZ * NG
HALF = NZ // 2
PAR, SHARE, D = 8, 32, 1024
COLS = PAR * SHARE
FLOOR = -1e30
TEMP = 1.0 / 32.0


def dz_of(s):
    odd = s % 2
    d = HALF - (s + 1) // 2
    return odd * d + (1 - odd) * (NZ - d)


def sdz(s):
    odd = lax.rem(s, 2)
    d = HALF - lax.div(s + 1, 2)
    return odd * d + (1 - odd) * (NZ - d)


def mult(x, m):
    return pl.multiple_of(x, m)


def iota(shape, dim):
    return lax.broadcasted_iota(jnp.int32, shape, dim)


def kernel(
    emb, listing, counting, parent, ccount, cent,
    out, energy,
    stage, tiles, xg, rows_f, xs, panel, norms, lg, resp, wsum,
    meta_o, zb, sb, yb, mx, xm,
    sx, rx, est, eb, fs, fb, fo,
    pan_sem, zss, zrs, xss, xrl, xrr, xrf, mss, mzr, myr, mxr, sss, srs, ess, ezr, eyr,
):
    r = lax.axis_index("rows")
    q = lax.axis_index("rep")
    z = lax.div(r, NG)
    g = lax.rem(r, NG)
    right = lax.rem(q + 1, NQ)
    left = lax.rem(q + 3, NQ)
    opp = lax.rem(q + 2, NQ)

    def remote(src, dst, ss, rs, dev):
        return pltpu.make_async_remote_copy(
            src_ref=src, dst_ref=dst, send_sem=ss, recv_sem=rs, device_id=dev, device_id_type=MESH
        )

    barrier = pltpu.get_barrier_semaphore()

    @pl.loop(1, NR)
    def _(i):
        pl.semaphore_signal(
            barrier, inc=1, device_id=(lax.rem(r + i, NR), q), device_id_type=MESH
        )

    for peer in (right, left, opp):
        pl.semaphore_signal(barrier, inc=1, device_id=(r, peer), device_id_type=MESH)

    load = pltpu.make_async_copy(cent.at[:, pl.ds(mult(q * SHARE, SHARE), SHARE), :], panel, pan_sem)
    load.start()

    lane = iota((NR, NR), 1)
    row_i = iota((NR, NR), 0)
    count_col = jnp.sum(jnp.where(lane == row_i, counting[...].astype(F32), 0.0), axis=1, keepdims=True)
    par_row = lax.rem(parent[...], PAR).astype(F32)
    hots = []
    meta = jnp.zeros((NR, NR), F32)
    for j in range(2):
        hot = (lane == listing[:, j : j + 1]) & (count_col > j)
        hots.append(hot)
        code = jnp.sum(jnp.where(hot, par_row + 1.0, 0.0), axis=1, keepdims=True)
        meta = meta + jnp.where(lax.rem(lane, 16) == g * 2 + j, code, 0.0)
        picked = jnp.dot(hot.astype(BF16), emb[...], preferred_element_type=F32)
        for k in range(8):
            stage[pl.ds(j * 8 + k, NR, stride=16), :] = picked[:, 128 * k : 128 * (k + 1)]
    tiles[...] = stage[...].astype(BF16)
    meta_o[...] = meta

    load.wait()
    for p in range(PAR):
        wide = panel[p].astype(F32)
        norms[p * SHARE : (p + 1) * SHARE, :] = jnp.sum(wide * wide, axis=1, keepdims=True)

    pl.semaphore_wait(barrier, NR - 1 + NQ - 1)

    def send_rows(s, i):
        zt = lax.rem(z + sdz(s), NZ)
        o = zt * NG + lax.rem(g + i, NG)
        remote(
            tiles.at[pl.ds(mult(o * 16, 16), 16)],
            xg.at[pl.ds(mult((s * NQ + q) * 128 + g * 16, 16), 16)],
            zss, zrs.at[s], (o, q),
        ).start()

    def send_steps(first, last):
        @pl.loop(first, last)
        def _(s):
            @pl.loop(0, NG)
            def _(i):
                send_rows(s, i)

    send_steps(0, 2)

    @pl.loop(0, NZ - 1)
    def _(s):
        zt = lax.rem(z + sdz(s), NZ)
        remote(
            meta_o.at[pl.ds(mult(zt * NG, 8), 8)], zb.at[pl.ds(mult(s * 8, 8), 8)],
            mss, mzr, (zt * NG + g, q),
        ).start()

    send_steps(2, NZ - 1)

    @pl.loop(1, NG)
    def _(i):
        send_rows(NZ - 1, i)

    xg[pl.ds(mult(((NZ - 1) * NQ + q) * 128 + g * 16, 16), 16), :] = tiles[pl.ds(mult(r * 16, 16), 16), :]
    zb[(NZ - 1) * 8 :, :] = meta_o[pl.ds(mult(z * 8, 8), 8), :]

    def chunk(t, qq):
        return xg.at[pl.ds(mult((t * NQ + qq) * 128, 128), 128)]

    def step(s):
        @pl.when(s < NZ)
        def _():
            @pl.when(s < NZ - 1)
            def _():
                remote(chunk(s, q), chunk(s, q), zss, zrs.at[s], (r, right)).wait_recv()

            @pl.when(s == NZ - 1)
            def _():
                part = xg.at[pl.ds(0, 112)]
                remote(part, part, zss, zrs.at[s], (r, right)).wait_recv()

            remote(chunk(s, q), chunk(s, q), xss, xrl.at[s], (r, right)).start()
            remote(chunk(s, q), chunk(s, q), xss, xrr.at[s], (r, left)).start()

        @pl.when((s >= 1) & (s <= NZ))
        def _():
            t = s - 1
            remote(chunk(t, q), chunk(t, left), xss, xrl.at[t], (r, right)).wait_recv()
            remote(chunk(t, q), chunk(t, right), xss, xrr.at[t], (r, left)).wait_recv()

            @pl.when(lax.rem(t, 2) == 0)
            def _():
                remote(chunk(t, left), chunk(t, left), xss, xrf.at[t], (r, right)).start()

            @pl.when(lax.rem(t, 2) == 1)
            def _():
                remote(chunk(t, right), chunk(t, right), xss, xrf.at[t], (r, left)).start()

        @pl.when(s >= 2)
        def _():
            t = s - 2
            remote(chunk(t, q), chunk(t, opp), xss, xrf.at[t], (r, right)).wait_recv()
            half = lax.div(t, HALF)
            place = half * 512 + lax.rem(t, HALF) * 16
            for qq in range(NQ):
                rows_f[qq * 128 : (qq + 1) * 128, :] = xg[
                    pl.ds(mult((t * NQ + qq) * 128, 128), 128), :
                ].astype(F32)
                for k in range(8):
                    xs[pl.ds(mult(place + qq * 128, 16), 16), 128 * k : 128 * (k + 1)] = rows_f[
                        pl.ds(qq * 128 + k, 16, stride=8), :
                    ].astype(BF16)

    pl.loop(0, 4)(step)

    mate = meta_o.at[pl.ds(0, 120)]
    remote(mate, zb.at[pl.ds(0, 120)], mss, mzr, (r, right)).wait_recv()
    for gg in range(NG):
        sb[gg * 16 : (gg + 1) * 16, :] = zb[pl.ds(gg, 16, stride=8), :]

    @pl.loop(1, NG)
    def _(i):
        gt = lax.rem(g + i, NG)
        remote(
            sb.at[pl.ds(mult(gt * 16, 16), 16)], yb.at[pl.ds(mult(g * 16, 16), 16)],
            mss, myr, (z * NG + gt, q),
        ).start()

    yb[pl.ds(mult(g * 16, 16), 16), :] = sb[pl.ds(mult(g * 16, 16), 16), :]

    pl.loop(4, 6)(step)

    mate = sb.at[pl.ds(0, 112)]
    remote(mate, yb.at[pl.ds(0, 112)], mss, myr, (r, right)).wait_recv()
    slot = yb[0:16, :]
    for gg in range(1, NG):
        slot = slot + yb[gg * 16 : (gg + 1) * 16, :]
    sl = iota((16, 128), 0)
    ln = lax.div(iota((16, 128), 1), 16)
    for h in range(2):
        mx[h : h + 1, :] = jnp.sum(jnp.where(sl == h * HALF + ln, slot, 0.0), axis=0, keepdims=True)
    mx[2:8, :] = jnp.zeros((6, 128), F32)
    for k, peer in enumerate((right, left, opp)):
        remote(mx, xm.at[pl.ds(mult(q * 8, 8), 8)], mss, mxr, (r, peer)).start()
    xm[pl.ds(mult(q * 8, 8), 8), :] = mx[...]

    pl.loop(6, 8)(step)

    mate = xm.at[pl.ds(0, 24)]
    remote(mate, mate, mss, mxr, (r, right)).wait_recv()

    kid = iota((SHARE, 1), 0) + q * SHARE

    def codes(h):
        return jnp.concatenate([xm[qq * 8 + h : qq * 8 + h + 1, :] for qq in range(NQ)], axis=1)

    def local_softmax(it, h):
        lg[...] = lax.dot_general(
            panel[...].reshape(COLS, D), xs[h * 512 : (h + 1) * 512, :],
            (((1,), (1,)), ((), ())), preferred_element_type=F32,
        )
        code = codes(h)
        top = jnp.full((1, 512), FLOOR, F32)
        for p in range(PAR):
            rows = slice(p * SHARE, (p + 1) * SHARE)
            allowed = (code == p + 1.0) & (kid < ccount[p])
            logits = jnp.where(allowed, (2.0 * lg[rows, :] - norms[rows, :]) * TEMP, FLOOR)
            lg[rows, :] = logits
            top = jnp.maximum(top, jnp.max(logits, axis=0, keepdims=True))
        total = jnp.zeros((1, 512), F32)
        for p in range(PAR):
            rows = slice(p * SHARE, (p + 1) * SHARE)
            logits = lg[rows, :]
            terms = jnp.where(logits > 0.5 * FLOOR, jnp.exp(logits - top), 0.0)
            resp[rows, h * 512 : (h + 1) * 512] = terms
            total = total + jnp.sum(terms, axis=0, keepdims=True)
        base = (it * 2 + h) * 8
        for qq in range(NQ):
            sx[base + qq : base + qq + 1, :] = top[:, qq * 128 : (qq + 1) * 128]
            sx[base + 4 + qq : base + 5 + qq, :] = total[:, qq * 128 : (qq + 1) * 128]
        for k, peer in enumerate((right, left, opp)):
            remote(
                sx.at[pl.ds(base, 8)], rx.at[pl.ds((it * 2 + h) * 24 + k * 8, 8)],
                sss, srs.at[(it * 2 + h) * 3 + k], (r, peer),
            ).start()

    def whole_softmax(it, h):
        base = (it * 2 + h) * 8
        mine = sx[base : base + 8, :]
        top = mine[0:4]
        others = []
        for k in range(3):
            at = (it * 2 + h) * 24 + k * 8
            remote(
                sx.at[pl.ds(base, 8)], rx.at[pl.ds(at, 8)], sss, srs.at[(it * 2 + h) * 3 + k], (r, right)
            ).wait_recv()
            others.append(rx[at : at + 8, :])
        for other in others:
            top = jnp.maximum(top, other[0:4])
        own = jnp.exp(mine[0:4] - top)
        total = mine[4:8] * own
        for other in others:
            total = total + other[4:8] * jnp.exp(other[0:4] - top)
        live = jnp.concatenate([xm[qq * 8 + h : qq * 8 + h + 1, :] for qq in range(NQ)], axis=0) > 0.5
        scale = jnp.where(live, own / total, 0.0)
        return scale, top + jnp.log(total)

    def weigh(h, scale):
        weights = jnp.zeros((COLS, 1), F32)
        for qq in range(NQ):
            cols = slice(h * 512 + qq * 128, h * 512 + (qq + 1) * 128)
            full = resp[:, cols] * scale[qq : qq + 1, :]
            resp[:, cols] = full
            weights = weights + jnp.sum(full, axis=1, keepdims=True)
        return weights

    pl.loop(8, 10)(step)
    local_softmax(0, 0)
    pl.loop(10, NZ + 2)(step)
    local_softmax(0, 1)

    for it in range(2):
        if it == 1:
            local_softmax(1, 0)
            local_softmax(1, 1)
        weights = jnp.zeros((COLS, 1), F32)
        for h in range(2):
            scale, full_energy = whole_softmax(it, h)
            if it == 1:
                own_row = jnp.sum(
                    jnp.where(iota((NQ, 128), 0) == q, full_energy, 0.0), axis=0, keepdims=True
                )
                est[h * 8 : (h + 1) * 8, :] = jnp.broadcast_to(own_row, (8, 128))

                @pl.loop(h * HALF, (h + 1) * HALF - h)
                def _(s):
                    zt = lax.rem(z + NZ - sdz(s), NZ)
                    remote(
                        est.at[pl.ds(h * 8, 8)], eb.at[pl.ds(mult(z * 8, 8), 8)],
                        ess, ezr, (zt * NG + g, q),
                    ).start()

            weights = weights + weigh(h, scale)
        inverse = 1.0 / (weights + 1.0)
        half_resp = resp[...].astype(BF16)
        square = jnp.zeros((COLS, 1), F32)
        for b in range(4):
            cols = slice(b * 256, (b + 1) * 256)
            sums = jnp.dot(half_resp, xs[:, cols], preferred_element_type=F32)
            old = panel[:, :, cols].reshape(COLS, 256).astype(F32)
            new = (sums + old) * inverse
            if it == 0:
                low = new.astype(BF16)
                panel[:, :, cols] = low.reshape(PAR, SHARE, 256)
                wide = low.astype(F32)
                square = square + jnp.sum(wide * wide, axis=1, keepdims=True)
            else:
                out[:, :, cols] = new.reshape(PAR, SHARE, 256)
        if it == 0:
            norms[...] = square

    mate = eb.at[pl.ds(0, 120)]
    remote(mate, mate, ess, ezr, (r, right)).wait_recv()
    eb[pl.ds(mult(z * 8, 8), 8), :] = est[8:16, :]
    fs[...] = eb[pl.ds(0, 16, stride=8), :]

    @pl.loop(1, NG)
    def _(i):
        gt = lax.rem(g + i, NG)
        remote(fs, fb.at[pl.ds(mult(g * 16, 16), 16)], ess, eyr, (z * NG + gt, q)).start()

    mate = fb.at[pl.ds(0, 112)]
    remote(mate, mate, ess, eyr, (r, right)).wait_recv()
    fb[pl.ds(mult(g * 16, 16), 16), :] = fs[...]
    for gg in range(NG):
        fo[pl.ds(gg, 16, stride=8), :] = fb[gg * 16 : (gg + 1) * 16, :]
    dz = lax.rem(lax.div(row_i, NG) + NZ - z, NZ)
    s_of = jnp.where(dz < HALF, NZ - 1 - 2 * dz, 2 * dz - NZ)
    at = lax.rem(s_of, HALF) * 16 + g * 2
    home = jnp.zeros((1, NR), F32)
    for j in range(2):
        hot = (lane == listing[:, j : j + 1]) & (count_col > j)
        value = jnp.sum(jnp.where(lane == at + j, fo[...], 0.0), axis=1, keepdims=True)
        home = home + jnp.sum(jnp.where(hot, value, 0.0), axis=0, keepdims=True)
    energy[...] = home

    def drain(ref, sem):
        remote(ref, ref, sem, pan_sem, (r, right)).wait_send()

    drain(tiles.at[pl.ds(0, 127 * 16)], zss)
    drain(xg.at[pl.ds(0, 48 * 128)], xss)
    drain(stage.at[pl.ds(0, 256)], mss)
    drain(rx, sss)
    drain(stage.at[pl.ds(0, 232)], ess)


def on_device(embeddings, parent_id, send_list, send_count, child_count, centroids):
    dma = pltpu.SemaphoreType.DMA
    vmem = pl.BlockSpec(memory_space=pltpu.VMEM)
    updated, row_energy = pl.pallas_call(
        kernel,
        name="refine",
        out_shape=(
            jax.ShapeDtypeStruct((PAR, SHARE, D), F32),
            jax.ShapeDtypeStruct((1, NR), F32),
        ),
        in_specs=[
            vmem, vmem, vmem, vmem,
            pl.BlockSpec(memory_space=pltpu.SMEM),
            pl.BlockSpec(memory_space=pl.ANY),
        ],
        out_specs=(vmem, vmem),
        scratch_shapes=[
            pltpu.VMEM((2048, 128), F32),
            pltpu.VMEM((2048, 128), BF16),
            pltpu.VMEM((64 * 128, 128), BF16),
            pltpu.VMEM((512, 128), F32),
            pltpu.VMEM((1024, D), BF16),
            pltpu.VMEM((PAR, SHARE, D), BF16),
            pltpu.VMEM((COLS, 1), F32),
            pltpu.VMEM((COLS, 512), F32),
            pltpu.VMEM((COLS, 1024), F32),
            pltpu.VMEM((8, 128), F32),
            pltpu.VMEM((128, 128), F32),
            pltpu.VMEM((128, 128), F32),
            pltpu.VMEM((128, 128), F32),
            pltpu.VMEM((128, 128), F32),
            pltpu.VMEM((8, 128), F32),
            pltpu.VMEM((32, 128), F32),
            pltpu.VMEM((32, 128), F32),
            pltpu.VMEM((96, 128), F32),
            pltpu.VMEM((16, 128), F32),
            pltpu.VMEM((128, 128), F32),
            pltpu.VMEM((16, 128), F32),
            pltpu.VMEM((128, 128), F32),
            pltpu.VMEM((128, 128), F32),
            dma, dma, dma((NZ,)), dma, dma((NZ,)), dma((NZ,)), dma((NZ,)),
            dma, dma, dma, dma,
            dma, dma((12,)),
            dma, dma, dma,
        ],
        compiler_params=pltpu.CompilerParams(
            collective_id=0, has_side_effects=True, vmem_limit_bytes=40 * 1024 * 1024
        ),
    )(
        embeddings,
        send_list[0],
        send_count,
        parent_id[None, :],
        child_count,
        centroids,
    )
    return (updated, row_energy[0])


def solution(mesh):
    in_specs = (
        P(("rows", "rep"), None),
        P(("rows", "rep")),
        P(("rows", "rep"), None, None),
        P(("rows", "rep"), None),
        P("rows"),
        P("rows", None, None),
    )
    out_specs = (P("rows", "rep", None), P(("rows", "rep")))
    return jax.shard_map(
        on_device, mesh=mesh, in_specs=in_specs, out_specs=out_specs, check_vma=False
    )
```

```python
import functools

import jax
import jax.numpy as jnp
from jax import lax
from jax.experimental import pallas as pl
from jax.experimental.pallas import tpu as pltpu
from jax.sharding import PartitionSpec as P

MESH = pl.DeviceIdType.MESH
F32 = jnp.float32
BF16 = jnp.bfloat16

NZ, NG, NQ = 16, 8, 4
NR = NZ * NG
HALF = NZ // 2
PAR, SHARE, D = 8, 32, 1024
COLS = PAR * SHARE
FLOOR = -1e30
LEAD, LAG1, LAG2 = 4, 2, 4
TEMP = 1.0 / 32.0


def sdz(s):
    odd = lax.rem(s, 2)
    return odd * lax.div(s + 1, 2) + (1 - odd) * (NZ - lax.div(s, 2))


def mult(x, m):
    return pl.multiple_of(x, m)


def iota(shape, dim):
    return lax.broadcasted_iota(jnp.int32, shape, dim)


def kernel(
    emb_hbm, listing_hbm, counting_hbm, parent_hbm, ccount_hbm, cent,
    out, energy,
    emb, listing, counting, parent, ccount,
    stage, tiles, xg, rows_f, xs, panel, norms, lg, resp,
    meta_o, zb, sb, yb, mx, xm,
    sx, rx, est, eb, fs, fb, fo,
    in_sem, zss, zrs, xss, xrl, xrr, xrf, mss, mzr, myr, mxr, sss, srs, ess, ezr, eyr,
):
    r = lax.axis_index("rows")
    q = lax.axis_index("rep")
    z = lax.div(r, NG)
    g = lax.rem(r, NG)
    right = lax.rem(q + 1, NQ)
    left = lax.rem(q + 3, NQ)
    opp = lax.rem(q + 2, NQ)

    def remote(src, dst, ss, rs, dev):
        return pltpu.make_async_remote_copy(
            src_ref=src, dst_ref=dst, send_sem=ss, recv_sem=rs, device_id=dev, device_id_type=MESH
        )

    loads = [
        pltpu.make_async_copy(src, dst, in_sem.at[k])
        for k, (src, dst) in enumerate((
            (emb_hbm, emb),
            (listing_hbm, listing),
            (counting_hbm, counting),
            (parent_hbm, parent),
            (ccount_hbm, ccount),
            (cent.at[:, pl.ds(mult(q * SHARE, SHARE), SHARE), :], panel),
        ))
    ]
    for load in loads:
        load.start()

    barrier = pltpu.get_barrier_semaphore()

    @pl.loop(1, NR)
    def _(i):
        pl.semaphore_signal(
            barrier, inc=1, device_id=(lax.rem(r + i, NR), q), device_id_type=MESH
        )

    for peer in (right, left, opp):
        pl.semaphore_signal(barrier, inc=1, device_id=(r, peer), device_id_type=MESH)

    for load in loads:
        load.wait()

    lane = iota((NR, NR), 1)
    row_i = iota((NR, NR), 0)
    count_col = jnp.sum(jnp.where(lane == row_i, counting[...].astype(F32), 0.0), axis=1, keepdims=True)
    par_row = lax.rem(parent[...], PAR).astype(F32)
    listed = []
    for j in range(2):
        wide = jnp.where(lane == row_i, listing[j : j + 1, :].astype(F32), 0.0)
        listed.append(jnp.sum(wide, axis=1, keepdims=True).astype(jnp.int32))
    meta = jnp.zeros((NR, NR), F32)
    for j in range(2):
        hot = (lane == listed[j]) & (count_col > j)
        code = jnp.sum(jnp.where(hot, par_row + 1.0, 0.0), axis=1, keepdims=True)
        meta = meta + jnp.where(lax.rem(lane, 16) == g * 2 + j, code, 0.0)
        picked = jnp.dot(hot.astype(BF16), emb[...], preferred_element_type=F32)
        for k in range(8):
            stage[pl.ds(j * 8 + k, NR, stride=16), :] = picked[:, 128 * k : 128 * (k + 1)]
    tiles[...] = stage[...].astype(BF16)
    meta_o[...] = meta

    for p in range(PAR):
        wide = panel[p].astype(F32)
        norms[p * SHARE : (p + 1) * SHARE, :] = jnp.sum(wide * wide, axis=1, keepdims=True)

    pl.semaphore_wait(barrier, NR - 1 + NQ - 1)

    def send_rows(s, i):
        zt = lax.rem(z + sdz(s), NZ)
        o = zt * NG + lax.rem(g + i, NG)
        remote(
            tiles.at[pl.ds(mult(o * 16, 16), 16)],
            xg.at[pl.ds(mult((s * NQ + q) * 128 + g * 16, 16), 16)],
            zss, zrs.at[s], (o, q),
        ).start()

    @pl.loop(1, NG)
    def _(i):
        send_rows(0, i)

    @pl.loop(1, NZ)
    def _(k):
        s = NZ - k
        zt = lax.rem(z + sdz(s), NZ)
        remote(
            meta_o.at[pl.ds(mult(zt * NG, 8), 8)], zb.at[pl.ds(mult(s * 8, 8), 8)],
            mss, mzr, (zt * NG + g, q),
        ).start()

    xg[pl.ds(mult(q * 128 + g * 16, 16), 16), :] = tiles[pl.ds(mult(r * 16, 16), 16), :]
    zb[0:8, :] = meta_o[pl.ds(mult(z * 8, 8), 8), :]

    def chunk(t, qq):
        return xg.at[pl.ds(mult((t * NQ + qq) * 128, 128), 128)]

    def step(s):
        @pl.when(s < NZ)
        def _():
            @pl.when(s > 0)
            def _():
                remote(chunk(s, q), chunk(s, q), zss, zrs.at[s], (r, right)).wait_recv()

            @pl.when(s == 0)
            def _():
                part = xg.at[pl.ds(0, 112)]
                remote(part, part, zss, zrs.at[s], (r, right)).wait_recv()

            remote(chunk(s, q), chunk(s, q), xss, xrl.at[s], (r, right)).start()
            remote(chunk(s, q), chunk(s, q), xss, xrr.at[s], (r, left)).start()

        @pl.when((s >= LAG1) & (s < NZ + LAG1))
        def _():
            t = s - LAG1
            remote(chunk(t, q), chunk(t, left), xss, xrl.at[t], (r, right)).wait_recv()
            remote(chunk(t, q), chunk(t, right), xss, xrr.at[t], (r, left)).wait_recv()

            @pl.when(lax.rem(t, 2) == 0)
            def _():
                remote(chunk(t, left), chunk(t, left), xss, xrf.at[t], (r, right)).start()

            @pl.when(lax.rem(t, 2) == 1)
            def _():
                remote(chunk(t, right), chunk(t, right), xss, xrf.at[t], (r, left)).start()

        @pl.when(s >= LAG2)
        def _():
            t = s - LAG2
            remote(chunk(t, q), chunk(t, opp), xss, xrf.at[t], (r, right)).wait_recv()
            half = lax.div(t, HALF)
            place = half * 512 + lax.rem(t, HALF) * 16
            for qq in range(NQ):
                rows_f[qq * 128 : (qq + 1) * 128, :] = xg[
                    pl.ds(mult((t * NQ + qq) * 128, 128), 128), :
                ].astype(F32)
                for k in range(8):
                    xs[pl.ds(mult(place + qq * 128, 16), 16), 128 * k : 128 * (k + 1)] = rows_f[
                        pl.ds(qq * 128 + k, 16, stride=8), :
                    ].astype(BF16)

    @pl.loop(1, NZ)
    def _(s):
        @pl.loop(0, NG)
        def _(i):
            send_rows(s, i)

        @pl.when(s >= LEAD)
        def _():
            step(s - LEAD)

    mate = meta_o.at[pl.ds(0, 120)]
    remote(mate, zb.at[pl.ds(0, 120)], mss, mzr, (r, right)).wait_recv()
    for gg in range(NG):
        sb[gg * 16 : (gg + 1) * 16, :] = zb[pl.ds(gg, 16, stride=8), :]

    @pl.loop(1, NG)
    def _(i):
        gt = lax.rem(g + i, NG)
        remote(
            sb.at[pl.ds(mult(gt * 16, 16), 16)], yb.at[pl.ds(mult(g * 16, 16), 16)],
            mss, myr, (z * NG + gt, q),
        ).start()

    yb[pl.ds(mult(g * 16, 16), 16), :] = sb[pl.ds(mult(g * 16, 16), 16), :]

    pl.loop(NZ - LEAD, NZ - LEAD + 1)(step)

    mate = sb.at[pl.ds(0, 112)]
    remote(mate, yb.at[pl.ds(0, 112)], mss, myr, (r, right)).wait_recv()
    slot = yb[0:16, :]
    for gg in range(1, NG):
        slot = slot + yb[gg * 16 : (gg + 1) * 16, :]
    sl = iota((16, 128), 0)
    ln = lax.div(iota((16, 128), 1), 16)
    for h in range(2):
        mx[h : h + 1, :] = jnp.sum(jnp.where(sl == h * HALF + ln, slot, 0.0), axis=0, keepdims=True)
    mx[2:8, :] = jnp.zeros((6, 128), F32)
    for k, peer in enumerate((right, left, opp)):
        remote(mx, xm.at[pl.ds(mult(q * 8, 8), 8)], mss, mxr, (r, peer)).start()
    xm[pl.ds(mult(q * 8, 8), 8), :] = mx[...]

    pl.loop(NZ - LEAD + 1, NZ - 1)(step)

    mate = xm.at[pl.ds(0, 24)]
    remote(mate, mate, mss, mxr, (r, right)).wait_recv()

    kid = iota((SHARE, 1), 0) + q * SHARE

    def codes(h):
        return jnp.concatenate([xm[qq * 8 + h : qq * 8 + h + 1, :] for qq in range(NQ)], axis=1)

    def local_softmax(it, h):
        lg[...] = lax.dot_general(
            panel[...].reshape(COLS, D), xs[h * 512 : (h + 1) * 512, :],
            (((1,), (1,)), ((), ())), preferred_element_type=F32,
        )
        code = codes(h)
        top = jnp.full((1, 512), FLOOR, F32)
        for p in range(PAR):
            rows = slice(p * SHARE, (p + 1) * SHARE)
            allowed = (code == p + 1.0) & (kid < ccount[p])
            logits = jnp.where(allowed, (2.0 * lg[rows, :] - norms[rows, :]) * TEMP, FLOOR)
            lg[rows, :] = logits
            top = jnp.maximum(top, jnp.max(logits, axis=0, keepdims=True))
        total = jnp.zeros((1, 512), F32)
        for p in range(PAR):
            rows = slice(p * SHARE, (p + 1) * SHARE)
            logits = lg[rows, :]
            terms = jnp.where(logits > 0.5 * FLOOR, jnp.exp(logits - top), 0.0)
            resp[rows, h * 512 : (h + 1) * 512] = terms
            total = total + jnp.sum(terms, axis=0, keepdims=True)
        base = (it * 2 + h) * 8
        for qq in range(NQ):
            sx[base + qq : base + qq + 1, :] = top[:, qq * 128 : (qq + 1) * 128]
            sx[base + 4 + qq : base + 5 + qq, :] = total[:, qq * 128 : (qq + 1) * 128]
        for k, peer in enumerate((right, left, opp)):
            remote(
                sx.at[pl.ds(base, 8)], rx.at[pl.ds((it * 2 + h) * 24 + k * 8, 8)],
                sss, srs.at[(it * 2 + h) * 3 + k], (r, peer),
            ).start()

    def whole_softmax(it, h):
        base = (it * 2 + h) * 8
        mine = sx[base : base + 8, :]
        top = mine[0:4]
        others = []
        for k in range(3):
            at = (it * 2 + h) * 24 + k * 8
            remote(
                sx.at[pl.ds(base, 8)], rx.at[pl.ds(at, 8)], sss, srs.at[(it * 2 + h) * 3 + k], (r, right)
            ).wait_recv()
            others.append(rx[at : at + 8, :])
        for other in others:
            top = jnp.maximum(top, other[0:4])
        own = jnp.exp(mine[0:4] - top)
        total = mine[4:8] * own
        for other in others:
            total = total + other[4:8] * jnp.exp(other[0:4] - top)
        live = jnp.concatenate([xm[qq * 8 + h : qq * 8 + h + 1, :] for qq in range(NQ)], axis=0) > 0.5
        scale = jnp.where(live, own / total, 0.0)
        return scale, top + jnp.log(total)

    def weigh(h, scale):
        weights = jnp.zeros((COLS, 1), F32)
        for qq in range(NQ):
            cols = slice(h * 512 + qq * 128, h * 512 + (qq + 1) * 128)
            full = resp[:, cols] * scale[qq : qq + 1, :]
            resp[:, cols] = full
            weights = weights + jnp.sum(full, axis=1, keepdims=True)
        return weights

    local_softmax(0, 0)
    pl.loop(NZ - 1, NZ + LAG2)(step)
    local_softmax(0, 1)

    for it in range(2):
        if it == 1:
            local_softmax(1, 0)
            local_softmax(1, 1)
        weights = jnp.zeros((COLS, 1), F32)
        for h in range(2):
            scale, full_energy = whole_softmax(it, h)
            if it == 1:
                own_row = jnp.sum(
                    jnp.where(iota((NQ, 128), 0) == q, full_energy, 0.0), axis=0, keepdims=True
                )
                est[h * 8 : (h + 1) * 8, :] = jnp.broadcast_to(own_row, (8, 128))

                @pl.loop(1 - h, HALF)
                def _(k):
                    s = (h + 1) * HALF - 1 - k + (1 - h)
                    zt = lax.rem(z + NZ - sdz(s), NZ)
                    remote(
                        est.at[pl.ds(h * 8, 8)], eb.at[pl.ds(mult(z * 8, 8), 8)],
                        ess, ezr, (zt * NG + g, q),
                    ).start()

            weights = weights + weigh(h, scale)
        inverse = 1.0 / (weights + 1.0)
        half_resp = resp[...].astype(BF16)
        square = jnp.zeros((COLS, 1), F32)
        for b in range(4):
            cols = slice(b * 256, (b + 1) * 256)
            sums = jnp.dot(half_resp, xs[:, cols], preferred_element_type=F32)
            old = panel[:, :, cols].reshape(COLS, 256).astype(F32)
            new = (sums + old) * inverse
            if it == 0:
                low = new.astype(BF16)
                panel[:, :, cols] = low.reshape(PAR, SHARE, 256)
                wide = low.astype(F32)
                square = square + jnp.sum(wide * wide, axis=1, keepdims=True)
            else:
                out[:, :, cols] = new.reshape(PAR, SHARE, 256)
        if it == 0:
            norms[...] = square

    mate = eb.at[pl.ds(0, 120)]
    remote(mate, mate, ess, ezr, (r, right)).wait_recv()
    eb[pl.ds(mult(z * 8, 8), 8), :] = est[0:8, :]
    fs[...] = eb[pl.ds(0, 16, stride=8), :]

    @pl.loop(1, NG)
    def _(i):
        gt = lax.rem(g + i, NG)
        remote(fs, fb.at[pl.ds(mult(g * 16, 16), 16)], ess, eyr, (z * NG + gt, q)).start()

    mate = fb.at[pl.ds(0, 112)]
    remote(mate, mate, ess, eyr, (r, right)).wait_recv()
    fb[pl.ds(mult(g * 16, 16), 16), :] = fs[...]
    for gg in range(NG):
        fo[pl.ds(gg, 16, stride=8), :] = fb[gg * 16 : (gg + 1) * 16, :]
    dz = lax.rem(lax.div(row_i, NG) + NZ - z, NZ)
    s_of = jnp.where((dz >= 1) & (dz <= HALF), 2 * dz - 1, lax.rem(2 * (NZ - dz), 2 * NZ))
    at = lax.rem(s_of, HALF) * 16 + g * 2
    home = jnp.zeros((1, NR), F32)
    for j in range(2):
        hot = (lane == listed[j]) & (count_col > j)
        value = jnp.sum(jnp.where(lane == at + j, fo[...], 0.0), axis=1, keepdims=True)
        home = home + jnp.sum(jnp.where(hot, value, 0.0), axis=0, keepdims=True)
    energy[...] = home

    def drain(ref, sem):
        remote(ref, ref, sem, eyr, (r, right)).wait_send()

    drain(tiles.at[pl.ds(0, 127 * 16)], zss)
    drain(xg.at[pl.ds(0, 48 * 128)], xss)
    drain(stage.at[pl.ds(0, 256)], mss)
    drain(rx, sss)
    drain(stage.at[pl.ds(0, 232)], ess)


def on_device(embeddings, parent_id, send_list, send_count, child_count, centroids):
    dma = pltpu.SemaphoreType.DMA
    vmem = pl.BlockSpec(memory_space=pltpu.VMEM)
    updated, row_energy = pl.pallas_call(
        kernel,
        name="refine",
        out_shape=(
            jax.ShapeDtypeStruct((PAR, SHARE, D), F32),
            jax.ShapeDtypeStruct((1, NR), F32),
        ),
        in_specs=[pl.BlockSpec(memory_space=pltpu.HBM)] * 6,
        out_specs=(vmem, vmem),
        scratch_shapes=[
            pltpu.VMEM((NR, D), BF16),
            pltpu.VMEM((2, NR), jnp.int32),
            pltpu.VMEM((1, NR), jnp.int32),
            pltpu.VMEM((1, NR), jnp.int32),
            pltpu.SMEM((PAR,), jnp.int32),
            pltpu.VMEM((2048, 128), F32),
            pltpu.VMEM((2048, 128), BF16),
            pltpu.VMEM((64 * 128, 128), BF16),
            pltpu.VMEM((512, 128), F32),
            pltpu.VMEM((1024, D), BF16),
            pltpu.VMEM((PAR, SHARE, D), BF16),
            pltpu.VMEM((COLS, 1), F32),
            pltpu.VMEM((COLS, 512), F32),
            pltpu.VMEM((COLS, 1024), F32),
            pltpu.VMEM((128, 128), F32),
            pltpu.VMEM((128, 128), F32),
            pltpu.VMEM((128, 128), F32),
            pltpu.VMEM((128, 128), F32),
            pltpu.VMEM((8, 128), F32),
            pltpu.VMEM((32, 128), F32),
            pltpu.VMEM((32, 128), F32),
            pltpu.VMEM((96, 128), F32),
            pltpu.VMEM((16, 128), F32),
            pltpu.VMEM((128, 128), F32),
            pltpu.VMEM((16, 128), F32),
            pltpu.VMEM((128, 128), F32),
            pltpu.VMEM((128, 128), F32),
            dma((6,)), dma, dma((NZ,)), dma, dma((NZ,)), dma((NZ,)), dma((NZ,)),
            dma, dma, dma, dma,
            dma, dma((12,)),
            dma, dma, dma,
        ],
        compiler_params=pltpu.CompilerParams(
            collective_id=0, has_side_effects=True, vmem_limit_bytes=60 * 1024 * 1024
        ),
    )(
        embeddings,
        send_list[0].T,
        send_count,
        parent_id[None, :],
        child_count,
        centroids,
    )
    return (updated, row_energy[0])


def solution(mesh):
    in_specs = (
        P(("rows", "rep"), None),
        P(("rows", "rep")),
        P(("rows", "rep"), None, None),
        P(("rows", "rep"), None),
        P("rows"),
        P("rows", None, None),
    )
    out_specs = (P("rows", "rep", None), P(("rows", "rep")))
    return jax.shard_map(
        on_device, mesh=mesh, in_specs=in_specs, out_specs=out_specs, check_vma=False
    )
```

```python
import functools

import jax
import jax.numpy as jnp
from jax import lax
from jax.experimental import pallas as pl
from jax.experimental.pallas import tpu as pltpu
from jax.sharding import PartitionSpec as P

MESH = pl.DeviceIdType.MESH
F32 = jnp.float32
BF16 = jnp.bfloat16

NZ, NG, NQ = 16, 8, 4
NR = NZ * NG
HALF = NZ // 2
PAR, KIDS, SHARE, D = 8, 128, 32, 1024
COLS = PAR * SHARE
FLOOR = -1e30
LEAD, LAG = 8, 3
TEMP = 1.0 / 32.0


def sdz(s):
    odd = lax.rem(s, 2)
    return odd * lax.div(s + 1, 2) + (1 - odd) * (NZ - lax.div(s, 2))


def mult(x, m):
    return pl.multiple_of(x, m)


def iota(shape, dim):
    return lax.broadcasted_iota(jnp.int32, shape, dim)


def kernel(
    emb_hbm, listing_hbm, counting_hbm, parent_hbm, ccount_hbm, cent,
    out, energy,
    emb, listing, counting, parent, ccount,
    stage, tiles, xg, rows_f, xs, full, panel, norms, lg, terms, resp, wsum,
    meta_o, zb, sb, yb, mx, xm, mt,
    sx, rx, sc, est, eb, fs, fb, fo,
    in_sem, zss, zrs, xss, xrl, xrr, xrf, mss, mzr, myr, mxr, sss, srs, ess, ezr, eyr,
):
    r = lax.axis_index("rows")
    q = lax.axis_index("rep")
    z = lax.div(r, NG)
    g = lax.rem(r, NG)
    right = lax.rem(q + 1, NQ)
    left = lax.rem(q + 3, NQ)
    opp = lax.rem(q + 2, NQ)

    def remote(src, dst, ss, rs, dev):
        return pltpu.make_async_remote_copy(
            src_ref=src, dst_ref=dst, send_sem=ss, recv_sem=rs, device_id=dev, device_id_type=MESH
        )

    loads = [
        pltpu.make_async_copy(src, dst, in_sem.at[k])
        for k, (src, dst) in enumerate((
            (emb_hbm, emb),
            (listing_hbm, listing),
            (counting_hbm, counting),
            (parent_hbm, parent),
            (ccount_hbm, ccount),
            (cent.at[:, pl.ds(mult(q * SHARE, SHARE), SHARE), :], panel),
            (cent, full),
        ))
    ]
    for load in loads:
        load.start()

    barrier = pltpu.get_barrier_semaphore()

    @pl.loop(1, NR)
    def _(i):
        pl.semaphore_signal(
            barrier, inc=1, device_id=(lax.rem(r + i, NR), q), device_id_type=MESH
        )

    for peer in (right, left, opp):
        pl.semaphore_signal(barrier, inc=1, device_id=(r, peer), device_id_type=MESH)

    for load in loads:
        load.wait()

    lane = iota((NR, NR), 1)
    row_i = iota((NR, NR), 0)
    count_col = jnp.sum(jnp.where(lane == row_i, counting[...].astype(F32), 0.0), axis=1, keepdims=True)
    par_row = lax.rem(parent[...], PAR).astype(F32)
    listed = []
    for j in range(2):
        wide = jnp.where(lane == row_i, listing[j : j + 1, :].astype(F32), 0.0)
        listed.append(jnp.sum(wide, axis=1, keepdims=True).astype(jnp.int32))
    meta = jnp.zeros((NR, NR), F32)
    for j in range(2):
        hot = (lane == listed[j]) & (count_col > j)
        code = jnp.sum(jnp.where(hot, par_row + 1.0, 0.0), axis=1, keepdims=True)
        meta = meta + jnp.where(lax.rem(lane, 16) == g * 2 + j, code, 0.0)
        picked = jnp.dot(hot.astype(BF16), emb[...], preferred_element_type=F32)
        for k in range(8):
            stage[pl.ds(j * 8 + k, NR, stride=16), :] = picked[:, 128 * k : 128 * (k + 1)]
    tiles[...] = stage[...].astype(BF16)
    meta_o[...] = meta

    kid = iota((KIDS, 1), 0)
    for p in range(PAR):
        wide = full[p].astype(F32)
        norm = jnp.sum(wide * wide, axis=1, keepdims=True) * TEMP
        norms[p * KIDS : (p + 1) * KIDS, :] = jnp.where(kid < ccount[p], norm, -FLOOR)

    pl.semaphore_wait(barrier, NR - 1 + NQ - 1)

    def send_rows(s, i):
        zt = lax.rem(z + sdz(s), NZ)
        o = zt * NG + lax.rem(g + i, NG)
        remote(
            tiles.at[pl.ds(mult(o * 16, 16), 16)],
            xg.at[pl.ds(mult((s * NQ + q) * 128 + g * 16, 16), 16)],
            zss, zrs.at[s], (o, q),
        ).start()

    @pl.loop(1, NG)
    def _(i):
        send_rows(0, i)

    xg[pl.ds(mult(q * 128 + g * 16, 16), 16), :] = tiles[pl.ds(mult(r * 16, 16), 16), :]
    zb[0:8, :] = meta_o[pl.ds(mult(z * 8, 8), 8), :]

    def chunk(t, qq):
        return xg.at[pl.ds(mult((t * NQ + qq) * 128, 128), 128)]

    def step(s):
        @pl.when(s < NZ)
        def _():
            @pl.when(s > 0)
            def _():
                remote(chunk(s, q), chunk(s, q), zss, zrs.at[s], (r, right)).wait_recv()

            @pl.when(s == 0)
            def _():
                part = xg.at[pl.ds(0, 112)]
                remote(part, part, zss, zrs.at[s], (r, right)).wait_recv()

            for rs, peer in ((xrl, right), (xrr, left), (xrf, opp)):
                remote(chunk(s, q), chunk(s, q), xss, rs.at[s], (r, peer)).start()

        @pl.when(s >= LAG)
        def _():
            t = s - LAG
            for rs, peer in ((xrl, left), (xrr, right), (xrf, opp)):
                remote(chunk(t, q), chunk(t, peer), xss, rs.at[t], (r, peer)).wait_recv()
            rows_f[...] = xg[pl.ds(mult(t * 512, 512), 512), :].astype(F32)
            for k in range(8):
                xs[pl.ds(mult(t * 64, 64), 64), 128 * k : 128 * (k + 1)] = rows_f[
                    pl.ds(k, 64, stride=8), :
                ].astype(BF16)

    def send_steps(first, last):
        @pl.loop(first, last)
        def _(s):
            @pl.loop(0, NG)
            def _(i):
                send_rows(s, i)

            @pl.when(s >= LEAD)
            def _():
                step(s - LEAD)

    send_steps(1, 5)

    @pl.loop(1, NZ)
    def _(k):
        s = NZ - k
        zt = lax.rem(z + sdz(s), NZ)
        remote(
            meta_o.at[pl.ds(mult(zt * NG, 8), 8)], zb.at[pl.ds(mult(s * 8, 8), 8)],
            mss, mzr, (zt * NG + g, q),
        ).start()

    send_steps(5, NZ)

    mate = meta_o.at[pl.ds(0, 120)]
    remote(mate, zb.at[pl.ds(0, 120)], mss, mzr, (r, right)).wait_recv()
    for gg in range(NG):
        sb[gg * 16 : (gg + 1) * 16, :] = zb[pl.ds(gg, 16, stride=8), :]

    @pl.loop(1, NG)
    def _(i):
        gt = lax.rem(g + i, NG)
        remote(
            sb.at[pl.ds(mult(gt * 16, 16), 16)], yb.at[pl.ds(mult(g * 16, 16), 16)],
            mss, myr, (z * NG + gt, q),
        ).start()

    yb[pl.ds(mult(g * 16, 16), 16), :] = sb[pl.ds(mult(g * 16, 16), 16), :]

    pl.loop(NZ - LEAD, NZ - LEAD + 1)(step)

    mate = sb.at[pl.ds(0, 112)]
    remote(mate, yb.at[pl.ds(0, 112)], mss, myr, (r, right)).wait_recv()
    slot = yb[0:16, :]
    for gg in range(1, NG):
        slot = slot + yb[gg * 16 : (gg + 1) * 16, :]
    sl = iota((16, 128), 0)
    ln = iota((16, 128), 1)
    mine = lax.rem(lax.div(ln, 16), NQ) == q
    for b in range(8):
        here = mine & (sl == 2 * b + lax.div(ln, 64))
        mx[b : b + 1, :] = jnp.sum(jnp.where(here, slot, 0.0), axis=0, keepdims=True)
    for k, peer in enumerate((right, left, opp)):
        remote(mx, xm.at[pl.ds(mult(q * 8, 8), 8)], mss, mxr, (r, peer)).start()
    xm[pl.ds(mult(q * 8, 8), 8), :] = mx[...]

    pl.loop(NZ - LEAD + 1, NZ - LEAD + 3)(step)

    mate = xm.at[pl.ds(0, 24)]
    remote(mate, mate, mss, mxr, (r, right)).wait_recv()

    mt[...] = xm[0:8, :] + xm[8:16, :] + xm[16:24, :] + xm[24:32, :]
    wsum[...] = jnp.zeros((COLS, 128), F32)

    def codes(b0, nb):
        return jnp.concatenate([mt[b : b + 1, :] for b in range(b0, b0 + nb)], axis=1)

    def gather_logits(code, kids, lanes):
        logits = jnp.full((kids, lanes), FLOOR, F32)
        for p in range(PAR):
            rows = slice(p * kids, (p + 1) * kids)
            value = lg[rows, 0:lanes] * (2.0 * TEMP) - norms[rows, :]
            logits = jnp.where(code == p + 1.0, value, logits)
        return logits

    def spread(code, b0, nb, share):
        for p in range(PAR):
            rows = slice(p * SHARE, (p + 1) * SHARE)
            value = jnp.where(code == p + 1.0, share, 0.0)
            resp[rows, b0 * 128 : (b0 + nb) * 128] = value.astype(BF16)
            total = value[:, 0:128]
            for b in range(1, nb):
                total = total + value[:, b * 128 : (b + 1) * 128]
            wsum[rows, :] = wsum[rows, :] + total

    def first_pass(b0, nb):
        lanes = nb * 128
        code = codes(b0, nb)
        lg[:, 0:lanes] = lax.dot_general(
            full[...].reshape(PAR * KIDS, D), xs[b0 * 128 : b0 * 128 + lanes, :],
            (((1,), (1,)), ((), ())), preferred_element_type=F32,
        )
        logits = gather_logits(code, KIDS, lanes)
        value = jnp.exp(logits - jnp.max(logits, axis=0, keepdims=True))
        total = jnp.sum(value, axis=0, keepdims=True)
        scale = jnp.where(code > 0.5, 1.0 / total, 0.0)
        terms[...] = value
        spread(code, b0, nb, terms[pl.ds(mult(q * SHARE, SHARE), SHARE), :] * scale)

    def update(last):
        inverse = 1.0 / (jnp.sum(wsum[...], axis=1, keepdims=True) + 1.0)
        square = jnp.zeros((COLS, 1), F32)
        for b in range(4):
            cols = slice(b * 256, (b + 1) * 256)
            sums = jnp.dot(resp[...], xs[:, cols], preferred_element_type=F32)
            old = panel[:, :, cols].reshape(COLS, 256).astype(F32)
            new = (sums + old) * inverse
            if last:
                out[:, :, cols] = new.reshape(PAR, SHARE, 256)
            else:
                low = new.astype(BF16)
                panel[:, :, cols] = low.reshape(PAR, SHARE, 256)
                wide = low.astype(F32)
                square = square + jnp.sum(wide * wide, axis=1, keepdims=True)
        return square

    first_pass(0, 2)
    pl.loop(NZ - 5, NZ - 4)(step)
    first_pass(2, 2)
    pl.loop(NZ - 4, NZ)(step)
    first_pass(4, 2)
    pl.loop(NZ, NZ + LAG)(step)
    first_pass(6, 2)
    square = update(False)

    kid = iota((SHARE, 1), 0) + q * SHARE
    for p in range(PAR):
        rows = slice(p * SHARE, (p + 1) * SHARE)
        norms[rows, :] = jnp.where(kid < ccount[p], square[rows] * TEMP, -FLOOR)
    wsum[...] = jnp.zeros((COLS, 128), F32)
    for h in range(4):
        code = codes(h * 2, 2)
        lg[0:COLS, 0:256] = lax.dot_general(
            panel[...].reshape(COLS, D), xs[h * 256 : (h + 1) * 256, :],
            (((1,), (1,)), ((), ())), preferred_element_type=F32,
        )
        logits = gather_logits(code, SHARE, 256)
        top = jnp.max(logits, axis=0, keepdims=True)
        value = jnp.exp(logits - top)
        total = jnp.sum(value, axis=0, keepdims=True)
        terms[h * SHARE : (h + 1) * SHARE, :] = value
        for b in range(2):
            sx[h * 2 + b : h * 2 + b + 1, :] = top[:, b * 128 : (b + 1) * 128]
            sx[8 + h * 2 + b : 9 + h * 2 + b, :] = total[:, b * 128 : (b + 1) * 128]
    peers = (right, left, opp)
    for k, peer in enumerate(peers):
        remote(sx, rx.at[pl.ds(k * 16, 16)], sss, srs.at[k], (r, peer)).start()
    tops, totals = [sx[0:8, :]], [sx[8:16, :]]
    for k in range(3):
        remote(sx, rx.at[pl.ds(k * 16, 16)], sss, srs.at[k], (r, right)).wait_recv()
        tops.append(rx[k * 16 : k * 16 + 8, :])
        totals.append(rx[k * 16 + 8 : k * 16 + 16, :])
    top = jnp.maximum(jnp.maximum(tops[0], tops[1]), jnp.maximum(tops[2], tops[3]))
    own = jnp.exp(tops[0] - top)
    total = totals[0] * own
    for k in range(1, 4):
        total = total + totals[k] * jnp.exp(tops[k] - top)
    est[...] = top + jnp.log(total)

    @pl.loop(1, NZ)
    def _(k):
        s = NZ - k
        zt = lax.rem(z + NZ - sdz(s), NZ)
        remote(est, eb.at[z], ess, ezr, (zt * NG + g, q)).start()

    sc[...] = jnp.where(mt[...] > 0.5, own / total, 0.0)
    for h in range(4):
        scale = jnp.concatenate([sc[h * 2 : h * 2 + 1, :], sc[h * 2 + 1 : h * 2 + 2, :]], axis=1)
        spread(codes(h * 2, 2), h * 2, 2, terms[h * SHARE : (h + 1) * SHARE, :] * scale)
    update(True)

    def step_of(dz):
        return jnp.where((dz >= 1) & (dz <= HALF), 2 * dz - 1, lax.rem(2 * (NZ - dz), 2 * NZ))

    mate = eb.at[pl.ds(0, NZ - 1)]
    remote(mate, mate, ess, ezr, (r, right)).wait_recv()
    eb[z] = est[...]
    shape = (NZ, 8, 128)
    block = lax.div(step_of(lax.rem(iota(shape, 0) + NZ - z, NZ)), 2)
    fs[...] = jnp.sum(jnp.where(iota(shape, 1) == block, eb[...], 0.0), axis=1)

    @pl.loop(1, NG)
    def _(i):
        gt = lax.rem(g + i, NG)
        remote(fs, fb.at[pl.ds(mult(g * 16, 16), 16)], ess, eyr, (z * NG + gt, q)).start()

    mate = fb.at[pl.ds(0, 112)]
    remote(mate, mate, ess, eyr, (r, right)).wait_recv()
    fb[pl.ds(mult(g * 16, 16), 16), :] = fs[...]
    for gg in range(NG):
        fo[pl.ds(gg, 16, stride=8), :] = fb[gg * 16 : (gg + 1) * 16, :]
    dz = lax.rem(lax.div(row_i, NG) + NZ - z, NZ)
    at = lax.rem(step_of(dz), 2) * 64 + q * 16 + g * 2
    home = jnp.zeros((1, NR), F32)
    for j in range(2):
        hot = (lane == listed[j]) & (count_col > j)
        value = jnp.sum(jnp.where(lane == at + j, fo[...], 0.0), axis=1, keepdims=True)
        home = home + jnp.sum(jnp.where(hot, value, 0.0), axis=0, keepdims=True)
    energy[...] = home

    def drain(ref, sem):
        remote(ref, ref, sem, eyr, (r, right)).wait_send()

    drain(tiles.at[pl.ds(0, 127 * 16)], zss)
    drain(xg.at[pl.ds(0, 48 * 128)], xss)
    drain(stage.at[pl.ds(0, 256)], mss)
    drain(rx, sss)
    drain(stage.at[pl.ds(0, 232)], ess)


def on_device(embeddings, parent_id, send_list, send_count, child_count, centroids):
    dma = pltpu.SemaphoreType.DMA
    vmem = pl.BlockSpec(memory_space=pltpu.VMEM)
    updated, row_energy = pl.pallas_call(
        kernel,
        name="refine",
        out_shape=(
            jax.ShapeDtypeStruct((PAR, SHARE, D), F32),
            jax.ShapeDtypeStruct((1, NR), F32),
        ),
        in_specs=[pl.BlockSpec(memory_space=pltpu.HBM)] * 6,
        out_specs=(vmem, vmem),
        scratch_shapes=[
            pltpu.VMEM((NR, D), BF16),
            pltpu.VMEM((2, NR), jnp.int32),
            pltpu.VMEM((1, NR), jnp.int32),
            pltpu.VMEM((1, NR), jnp.int32),
            pltpu.SMEM((PAR,), jnp.int32),
            pltpu.VMEM((2048, 128), F32),
            pltpu.VMEM((2048, 128), BF16),
            pltpu.VMEM((64 * 128, 128), BF16),
            pltpu.VMEM((512, 128), F32),
            pltpu.VMEM((1024, D), BF16),
            pltpu.VMEM((PAR, KIDS, D), BF16),
            pltpu.VMEM((PAR, SHARE, D), BF16),
            pltpu.VMEM((PAR * KIDS, 1), F32),
            pltpu.VMEM((PAR * KIDS, 256), F32),
            pltpu.VMEM((KIDS, 256), F32),
            pltpu.VMEM((COLS, 1024), BF16),
            pltpu.VMEM((COLS, 128), F32),
            pltpu.VMEM((128, 128), F32),
            pltpu.VMEM((128, 128), F32),
            pltpu.VMEM((128, 128), F32),
            pltpu.VMEM((128, 128), F32),
            pltpu.VMEM((8, 128), F32),
            pltpu.VMEM((32, 128), F32),
            pltpu.VMEM((8, 128), F32),
            pltpu.VMEM((16, 128), F32),
            pltpu.VMEM((48, 128), F32),
            pltpu.VMEM((8, 128), F32),
            pltpu.VMEM((8, 128), F32),
            pltpu.VMEM((NZ, 8, 128), F32),
            pltpu.VMEM((16, 128), F32),
            pltpu.VMEM((128, 128), F32),
            pltpu.VMEM((128, 128), F32),
            dma((7,)), dma, dma((NZ,)), dma, dma((NZ,)), dma((NZ,)), dma((NZ,)),
            dma, dma, dma, dma,
            dma, dma((3,)),
            dma, dma, dma,
        ],
        compiler_params=pltpu.CompilerParams(
            collective_id=0, has_side_effects=True, vmem_limit_bytes=60 * 1024 * 1024
        ),
    )(
        embeddings,
        send_list[0].T,
        send_count,
        parent_id[None, :],
        child_count,
        centroids,
    )
    return (updated, row_energy[0])


def solution(mesh):
    in_specs = (
        P(("rows", "rep"), None),
        P(("rows", "rep")),
        P(("rows", "rep"), None, None),
        P(("rows", "rep"), None),
        P("rows"),
        P("rows", None, None),
    )
    out_specs = (P("rows", "rep", None), P(("rows", "rep")))
    return jax.shard_map(
        on_device, mesh=mesh, in_specs=in_specs, out_specs=out_specs, check_vma=False
    )
```

```python
import functools

import jax
import jax.numpy as jnp
from jax import lax
from jax.experimental import pallas as pl
from jax.experimental.pallas import tpu as pltpu
from jax.sharding import PartitionSpec as P

MESH = pl.DeviceIdType.MESH
F32 = jnp.float32
BF16 = jnp.bfloat16

NZ, NG, NQ = 16, 8, 4
NR = NZ * NG
HALF = NZ // 2
PAR, KIDS, SHARE, D = 8, 128, 32, 1024
COLS = PAR * SHARE
FLOOR = -1e30
LEAD, LAG = 8, 3
TEMP = 1.0 / 32.0


def sdz(s):
    odd = lax.rem(s, 2)
    return odd * lax.div(s + 1, 2) + (1 - odd) * (NZ - lax.div(s, 2))


def mult(x, m):
    return pl.multiple_of(x, m)


def iota(shape, dim):
    return lax.broadcasted_iota(jnp.int32, shape, dim)


def kernel(
    emb_hbm, listing_hbm, counting_hbm, parent_hbm, ccount_hbm, cent,
    out, energy,
    emb, listing, counting, parent, ccount,
    stage, tiles, xg, rows_f, xs, full, panel, norms, lg, terms, resp, wsum,
    meta_o, zb, sb, yb, mx, xm, mt,
    sx, rx, sc, est, eb, fs, fb, fo,
    up_sem, down_sem, in_sem, zss, zrs, xss, xrl, xrr, xrf, mss, mzr, myr, mxr, sss, srs, ess, ezr, eyr,
):
    r = lax.axis_index("rows")
    q = lax.axis_index("rep")
    z = lax.div(r, NG)
    g = lax.rem(r, NG)
    right = lax.rem(q + 1, NQ)
    left = lax.rem(q + 3, NQ)
    opp = lax.rem(q + 2, NQ)

    def remote(src, dst, ss, rs, dev):
        return pltpu.make_async_remote_copy(
            src_ref=src, dst_ref=dst, send_sem=ss, recv_sem=rs, device_id=dev, device_id_type=MESH
        )

    loads = [
        pltpu.make_async_copy(src, dst, in_sem.at[k])
        for k, (src, dst) in enumerate((
            (emb_hbm, emb),
            (listing_hbm, listing),
            (counting_hbm, counting),
            (parent_hbm, parent),
            (ccount_hbm, ccount),
            (cent.at[:, pl.ds(mult(q * SHARE, SHARE), SHARE), :], panel),
            (cent, full),
        ))
    ]
    for load in loads:
        load.start()

    barrier = pltpu.get_barrier_semaphore()
    up = (lax.rem(z + 1, NZ) * NG + g, q)
    down = (lax.rem(z + NZ - 1, NZ) * NG + g, q)
    for peer in (up, down, (r, right), (r, left), (r, opp)):
        pl.semaphore_signal(barrier, inc=1, device_id=peer, device_id_type=MESH)

    @pl.loop(1, NG)
    def _(i):
        mate = z * NG + lax.rem(g + i, NG)
        pl.semaphore_signal(barrier, inc=1, device_id=(mate, q), device_id_type=MESH)

    for load in loads:
        load.wait()

    lane = iota((NR, NR), 1)
    row_i = iota((NR, NR), 0)
    count_col = jnp.sum(jnp.where(lane == row_i, counting[...].astype(F32), 0.0), axis=1, keepdims=True)
    par_row = lax.rem(parent[...], PAR).astype(F32)
    listed = []
    for j in range(2):
        wide = jnp.where(lane == row_i, listing[j : j + 1, :].astype(F32), 0.0)
        listed.append(jnp.sum(wide, axis=1, keepdims=True).astype(jnp.int32))
    meta = jnp.zeros((NR, NR), F32)
    for j in range(2):
        hot = (lane == listed[j]) & (count_col > j)
        code = jnp.sum(jnp.where(hot, par_row + 1.0, 0.0), axis=1, keepdims=True)
        meta = meta + jnp.where(lax.rem(lane, 16) == g * 2 + j, code, 0.0)
        picked = jnp.dot(hot.astype(BF16), emb[...], preferred_element_type=F32)
        for k in range(8):
            stage[pl.ds(j * 8 + k, NR, stride=16), :] = picked[:, 128 * k : 128 * (k + 1)]
    tiles[...] = stage[...].astype(BF16)
    meta_o[...] = meta

    kid = iota((KIDS, 1), 0)
    for p in range(PAR):
        wide = full[p].astype(F32)
        norm = jnp.sum(wide * wide, axis=1, keepdims=True) * TEMP
        norms[p * KIDS : (p + 1) * KIDS, :] = jnp.where(kid < ccount[p], norm, -FLOOR)

    pl.semaphore_wait(barrier, 2 + NQ - 1 + NG - 1)

    pl.semaphore_signal(up_sem, inc=1, device_id=down, device_id_type=MESH)
    pl.semaphore_signal(down_sem, inc=1, device_id=up, device_id_type=MESH)

    def send_rows(s, i):
        zt = lax.rem(z + sdz(s), NZ)
        o = zt * NG + lax.rem(g + i, NG)
        remote(
            tiles.at[pl.ds(mult(o * 16, 16), 16)],
            xg.at[pl.ds(mult((s * NQ + q) * 128 + g * 16, 16), 16)],
            zss, zrs.at[s], (o, q),
        ).start()

    @pl.loop(1, NG)
    def _(i):
        send_rows(0, i)

    xg[pl.ds(mult(q * 128 + g * 16, 16), 16), :] = tiles[pl.ds(mult(r * 16, 16), 16), :]
    zb[0:8, :] = meta_o[pl.ds(mult(z * 8, 8), 8), :]

    def chunk(t, qq):
        return xg.at[pl.ds(mult((t * NQ + qq) * 128, 128), 128)]

    def step(s):
        @pl.when(s < NZ)
        def _():
            @pl.when(s > 0)
            def _():
                remote(chunk(s, q), chunk(s, q), zss, zrs.at[s], (r, right)).wait_recv()

            @pl.when(s == 0)
            def _():
                part = xg.at[pl.ds(0, 112)]
                remote(part, part, zss, zrs.at[s], (r, right)).wait_recv()

            for rs, peer in ((xrl, right), (xrr, left), (xrf, opp)):
                remote(chunk(s, q), chunk(s, q), xss, rs.at[s], (r, peer)).start()

        @pl.when(s >= LAG)
        def _():
            t = s - LAG
            for rs, peer in ((xrl, left), (xrr, right), (xrf, opp)):
                remote(chunk(t, q), chunk(t, peer), xss, rs.at[t], (r, peer)).wait_recv()
            rows_f[...] = xg[pl.ds(mult(t * 512, 512), 512), :].astype(F32)
            for k in range(8):
                xs[pl.ds(mult(t * 64, 64), 64), 128 * k : 128 * (k + 1)] = rows_f[
                    pl.ds(k, 64, stride=8), :
                ].astype(BF16)

    def send_steps(first, last):
        @pl.loop(first, last)
        def _(s):
            @pl.loop(0, NG)
            def _(i):
                send_rows(s, i)

            @pl.when(s >= LEAD)
            def _():
                step(s - LEAD)

    def send_parents(s):
        zt = lax.rem(z + sdz(s), NZ)
        remote(
            meta_o.at[pl.ds(mult(zt * NG, 8), 8)], zb.at[pl.ds(mult(s * 8, 8), 8)],
            mss, mzr, (zt * NG + g, q),
        ).start()

    @pl.loop(1, HALF)
    def _(d):
        pl.semaphore_wait(up_sem, 1)
        pl.semaphore_signal(up_sem, inc=1, device_id=down, device_id_type=MESH)
        pl.semaphore_wait(down_sem, 1)

        @pl.when(d < HALF - 1)
        def _():
            pl.semaphore_signal(down_sem, inc=1, device_id=up, device_id_type=MESH)

        send_parents(2 * d - 1)
        send_parents(2 * d)

        @pl.loop(0, NG)
        def _(i):
            send_rows(d, i)

    pl.semaphore_wait(up_sem, 1)
    send_parents(NZ - 1)
    send_steps(HALF, NZ)

    mate = meta_o.at[pl.ds(0, 120)]
    remote(mate, zb.at[pl.ds(0, 120)], mss, mzr, (r, right)).wait_recv()
    for gg in range(NG):
        sb[gg * 16 : (gg + 1) * 16, :] = zb[pl.ds(gg, 16, stride=8), :]

    @pl.loop(1, NG)
    def _(i):
        gt = lax.rem(g + i, NG)
        remote(
            sb.at[pl.ds(mult(gt * 16, 16), 16)], yb.at[pl.ds(mult(g * 16, 16), 16)],
            mss, myr, (z * NG + gt, q),
        ).start()

    yb[pl.ds(mult(g * 16, 16), 16), :] = sb[pl.ds(mult(g * 16, 16), 16), :]

    pl.loop(NZ - LEAD, NZ - LEAD + 1)(step)

    mate = sb.at[pl.ds(0, 112)]
    remote(mate, yb.at[pl.ds(0, 112)], mss, myr, (r, right)).wait_recv()
    slot = yb[0:16, :]
    for gg in range(1, NG):
        slot = slot + yb[gg * 16 : (gg + 1) * 16, :]
    sl = iota((16, 128), 0)
    ln = iota((16, 128), 1)
    mine = lax.rem(lax.div(ln, 16), NQ) == q
    for b in range(8):
        here = mine & (sl == 2 * b + lax.div(ln, 64))
        mx[b : b + 1, :] = jnp.sum(jnp.where(here, slot, 0.0), axis=0, keepdims=True)
    for k, peer in enumerate((right, left, opp)):
        remote(mx, xm.at[pl.ds(mult(q * 8, 8), 8)], mss, mxr, (r, peer)).start()
    xm[pl.ds(mult(q * 8, 8), 8), :] = mx[...]

    pl.loop(NZ - LEAD + 1, NZ - LEAD + 3)(step)

    mate = xm.at[pl.ds(0, 24)]
    remote(mate, mate, mss, mxr, (r, right)).wait_recv()

    mt[...] = xm[0:8, :] + xm[8:16, :] + xm[16:24, :] + xm[24:32, :]
    wsum[...] = jnp.zeros((COLS, 128), F32)

    def codes(b0, nb):
        return jnp.concatenate([mt[b : b + 1, :] for b in range(b0, b0 + nb)], axis=1)

    def gather_logits(code, kids, lanes):
        logits = jnp.full((kids, lanes), FLOOR, F32)
        for p in range(PAR):
            rows = slice(p * kids, (p + 1) * kids)
            value = lg[rows, 0:lanes] * (2.0 * TEMP) - norms[rows, :]
            logits = jnp.where(code == p + 1.0, value, logits)
        return logits

    def spread(code, b0, nb, share):
        for p in range(PAR):
            rows = slice(p * SHARE, (p + 1) * SHARE)
            value = jnp.where(code == p + 1.0, share, 0.0)
            resp[rows, b0 * 128 : (b0 + nb) * 128] = value.astype(BF16)
            total = value[:, 0:128]
            for b in range(1, nb):
                total = total + value[:, b * 128 : (b + 1) * 128]
            wsum[rows, :] = wsum[rows, :] + total

    def first_pass(b0, nb):
        lanes = nb * 128
        code = codes(b0, nb)
        lg[:, 0:lanes] = lax.dot_general(
            full[...].reshape(PAR * KIDS, D), xs[b0 * 128 : b0 * 128 + lanes, :],
            (((1,), (1,)), ((), ())), preferred_element_type=F32,
        )
        logits = gather_logits(code, KIDS, lanes)
        value = jnp.exp(logits - jnp.max(logits, axis=0, keepdims=True))
        total = jnp.sum(value, axis=0, keepdims=True)
        scale = jnp.where(code > 0.5, 1.0 / total, 0.0)
        terms[...] = value
        spread(code, b0, nb, terms[pl.ds(mult(q * SHARE, SHARE), SHARE), :] * scale)

    def update(last):
        inverse = 1.0 / (jnp.sum(wsum[...], axis=1, keepdims=True) + 1.0)
        square = jnp.zeros((COLS, 1), F32)
        for b in range(4):
            cols = slice(b * 256, (b + 1) * 256)
            sums = jnp.dot(resp[...], xs[:, cols], preferred_element_type=F32)
            old = panel[:, :, cols].reshape(COLS, 256).astype(F32)
            new = (sums + old) * inverse
            if last:
                out[:, :, cols] = new.reshape(PAR, SHARE, 256)
            else:
                low = new.astype(BF16)
                panel[:, :, cols] = low.reshape(PAR, SHARE, 256)
                wide = low.astype(F32)
                square = square + jnp.sum(wide * wide, axis=1, keepdims=True)
        return square

    first_pass(0, 2)
    pl.loop(NZ - 5, NZ - 4)(step)
    first_pass(2, 2)
    pl.loop(NZ - 4, NZ)(step)
    first_pass(4, 2)
    pl.loop(NZ, NZ + LAG)(step)
    first_pass(6, 2)
    square = update(False)

    kid = iota((SHARE, 1), 0) + q * SHARE
    for p in range(PAR):
        rows = slice(p * SHARE, (p + 1) * SHARE)
        norms[rows, :] = jnp.where(kid < ccount[p], square[rows] * TEMP, -FLOOR)
    wsum[...] = jnp.zeros((COLS, 128), F32)
    for h in range(4):
        code = codes(h * 2, 2)
        lg[0:COLS, 0:256] = lax.dot_general(
            panel[...].reshape(COLS, D), xs[h * 256 : (h + 1) * 256, :],
            (((1,), (1,)), ((), ())), preferred_element_type=F32,
        )
        logits = gather_logits(code, SHARE, 256)
        top = jnp.max(logits, axis=0, keepdims=True)
        value = jnp.exp(logits - top)
        total = jnp.sum(value, axis=0, keepdims=True)
        terms[h * SHARE : (h + 1) * SHARE, :] = value
        for b in range(2):
            sx[h * 2 + b : h * 2 + b + 1, :] = top[:, b * 128 : (b + 1) * 128]
            sx[8 + h * 2 + b : 9 + h * 2 + b, :] = total[:, b * 128 : (b + 1) * 128]
    peers = (right, left, opp)
    for k, peer in enumerate(peers):
        remote(sx, rx.at[pl.ds(k * 16, 16)], sss, srs.at[k], (r, peer)).start()
    tops, totals = [sx[0:8, :]], [sx[8:16, :]]
    for k in range(3):
        remote(sx, rx.at[pl.ds(k * 16, 16)], sss, srs.at[k], (r, right)).wait_recv()
        tops.append(rx[k * 16 : k * 16 + 8, :])
        totals.append(rx[k * 16 + 8 : k * 16 + 16, :])
    top = jnp.maximum(jnp.maximum(tops[0], tops[1]), jnp.maximum(tops[2], tops[3]))
    own = jnp.exp(tops[0] - top)
    total = totals[0] * own
    for k in range(1, 4):
        total = total + totals[k] * jnp.exp(tops[k] - top)
    est[...] = top + jnp.log(total)

    @pl.loop(1, NZ)
    def _(k):
        s = NZ - k
        zt = lax.rem(z + NZ - sdz(s), NZ)
        remote(est, eb.at[z], ess, ezr, (zt * NG + g, q)).start()

    sc[...] = jnp.where(mt[...] > 0.5, own / total, 0.0)
    for h in range(4):
        scale = jnp.concatenate([sc[h * 2 : h * 2 + 1, :], sc[h * 2 + 1 : h * 2 + 2, :]], axis=1)
        spread(codes(h * 2, 2), h * 2, 2, terms[h * SHARE : (h + 1) * SHARE, :] * scale)
    update(True)

    def step_of(dz):
        return jnp.where((dz >= 1) & (dz <= HALF), 2 * dz - 1, lax.rem(2 * (NZ - dz), 2 * NZ))

    mate = eb.at[pl.ds(0, NZ - 1)]
    remote(mate, mate, ess, ezr, (r, right)).wait_recv()
    eb[z] = est[...]
    shape = (NZ, 8, 128)
    block = lax.div(step_of(lax.rem(iota(shape, 0) + NZ - z, NZ)), 2)
    fs[...] = jnp.sum(jnp.where(iota(shape, 1) == block, eb[...], 0.0), axis=1)

    @pl.loop(1, NG)
    def _(i):
        gt = lax.rem(g + i, NG)
        remote(fs, fb.at[pl.ds(mult(g * 16, 16), 16)], ess, eyr, (z * NG + gt, q)).start()

    mate = fb.at[pl.ds(0, 112)]
    remote(mate, mate, ess, eyr, (r, right)).wait_recv()
    fb[pl.ds(mult(g * 16, 16), 16), :] = fs[...]
    for gg in range(NG):
        fo[pl.ds(gg, 16, stride=8), :] = fb[gg * 16 : (gg + 1) * 16, :]
    dz = lax.rem(lax.div(row_i, NG) + NZ - z, NZ)
    at = lax.rem(step_of(dz), 2) * 64 + q * 16 + g * 2
    home = jnp.zeros((1, NR), F32)
    for j in range(2):
        hot = (lane == listed[j]) & (count_col > j)
        value = jnp.sum(jnp.where(lane == at + j, fo[...], 0.0), axis=1, keepdims=True)
        home = home + jnp.sum(jnp.where(hot, value, 0.0), axis=0, keepdims=True)
    energy[...] = home

    def drain(ref, sem):
        remote(ref, ref, sem, eyr, (r, right)).wait_send()

    drain(tiles.at[pl.ds(0, 127 * 16)], zss)
    drain(xg.at[pl.ds(0, 48 * 128)], xss)
    drain(stage.at[pl.ds(0, 256)], mss)
    drain(rx, sss)
    drain(stage.at[pl.ds(0, 232)], ess)


def on_device(embeddings, parent_id, send_list, send_count, child_count, centroids):
    dma = pltpu.SemaphoreType.DMA
    vmem = pl.BlockSpec(memory_space=pltpu.VMEM)
    updated, row_energy = pl.pallas_call(
        kernel,
        name="refine",
        out_shape=(
            jax.ShapeDtypeStruct((PAR, SHARE, D), F32),
            jax.ShapeDtypeStruct((1, NR), F32),
        ),
        in_specs=[pl.BlockSpec(memory_space=pltpu.HBM)] * 6,
        out_specs=(vmem, vmem),
        scratch_shapes=[
            pltpu.VMEM((NR, D), BF16),
            pltpu.VMEM((2, NR), jnp.int32),
            pltpu.VMEM((1, NR), jnp.int32),
            pltpu.VMEM((1, NR), jnp.int32),
            pltpu.SMEM((PAR,), jnp.int32),
            pltpu.VMEM((2048, 128), F32),
            pltpu.VMEM((2048, 128), BF16),
            pltpu.VMEM((64 * 128, 128), BF16),
            pltpu.VMEM((512, 128), F32),
            pltpu.VMEM((1024, D), BF16),
            pltpu.VMEM((PAR, KIDS, D), BF16),
            pltpu.VMEM((PAR, SHARE, D), BF16),
            pltpu.VMEM((PAR * KIDS, 1), F32),
            pltpu.VMEM((PAR * KIDS, 256), F32),
            pltpu.VMEM((KIDS, 256), F32),
            pltpu.VMEM((COLS, 1024), BF16),
            pltpu.VMEM((COLS, 128), F32),
            pltpu.VMEM((128, 128), F32),
            pltpu.VMEM((128, 128), F32),
            pltpu.VMEM((128, 128), F32),
            pltpu.VMEM((128, 128), F32),
            pltpu.VMEM((8, 128), F32),
            pltpu.VMEM((32, 128), F32),
            pltpu.VMEM((8, 128), F32),
            pltpu.VMEM((16, 128), F32),
            pltpu.VMEM((48, 128), F32),
            pltpu.VMEM((8, 128), F32),
            pltpu.VMEM((8, 128), F32),
            pltpu.VMEM((NZ, 8, 128), F32),
            pltpu.VMEM((16, 128), F32),
            pltpu.VMEM((128, 128), F32),
            pltpu.VMEM((128, 128), F32),
            pltpu.SemaphoreType.REGULAR, pltpu.SemaphoreType.REGULAR,
            dma((7,)), dma, dma((NZ,)), dma, dma((NZ,)), dma((NZ,)), dma((NZ,)),
            dma, dma, dma, dma,
            dma, dma((3,)),
            dma, dma, dma,
        ],
        compiler_params=pltpu.CompilerParams(
            collective_id=0, has_side_effects=True, vmem_limit_bytes=60 * 1024 * 1024
        ),
    )(
        embeddings,
        send_list[0].T,
        send_count,
        parent_id[None, :],
        child_count,
        centroids,
    )
    return (updated, row_energy[0])


def solution(mesh):
    in_specs = (
        P(("rows", "rep"), None),
        P(("rows", "rep")),
        P(("rows", "rep"), None, None),
        P(("rows", "rep"), None),
        P("rows"),
        P("rows", None, None),
    )
    out_specs = (P("rows", "rep", None), P(("rows", "rep")))
    return jax.shard_map(
        on_device, mesh=mesh, in_specs=in_specs, out_specs=out_specs, check_vma=False
    )
```

```python
import jax
import jax.numpy as jnp
from jax import lax
from jax.experimental import pallas as pl
from jax.experimental.pallas import tpu as pltpu
from jax.sharding import PartitionSpec as P

MESH = pl.DeviceIdType.MESH
F32 = jnp.float32
BF16 = jnp.bfloat16

NZ, NG, NQ = 16, 8, 4
NR = NZ * NG
HALF = NZ // 2
PAR, KIDS, SHARE, D = 8, 128, 32, 1024
COLS = PAR * SHARE
FLOOR = -1e30
LEAD, LAG = 8, 3
TEMP = 1.0 / 32.0


def sdz(s):
    odd = lax.rem(s, 2)
    return odd * lax.div(s + 1, 2) + (1 - odd) * (NZ - lax.div(s, 2))


def mult(x, m):
    return pl.multiple_of(x, m)


def iota(shape, dim):
    return lax.broadcasted_iota(jnp.int32, shape, dim)


def kernel(
    emb_hbm, listing_hbm, counting_hbm, parent_hbm, ccount_hbm, cent,
    out_hbm, energy,
    out, out_sem, emb, listing, counting, parent, ccount,
    stage, tiles, xg, rows_f, xs, full, panel, norms, lg, terms, resp, wsum,
    meta_o, zb, sb, yb, mx, xm, mt,
    sx, rx, sc, est, eb, fs, fb, fo,
    up_sem, down_sem, in_sem, zss, zrs, xss, xrl, xrr, xrf, mss, mzr, myr, mxr, sss, srs, ess, ezr, eyr,
):
    r = lax.axis_index("rows")
    q = lax.axis_index("rep")
    z = lax.div(r, NG)
    g = lax.rem(r, NG)
    right = lax.rem(q + 1, NQ)
    left = lax.rem(q + 3, NQ)
    opp = lax.rem(q + 2, NQ)

    def remote(src, dst, ss, rs, dev):
        return pltpu.make_async_remote_copy(
            src_ref=src, dst_ref=dst, send_sem=ss, recv_sem=rs, device_id=dev, device_id_type=MESH
        )

    loads = [
        pltpu.make_async_copy(src, dst, in_sem.at[k])
        for k, (src, dst) in enumerate((
            (emb_hbm, emb),
            (listing_hbm, listing),
            (counting_hbm, counting),
            (parent_hbm, parent),
            (ccount_hbm, ccount),
            (cent.at[:, pl.ds(mult(q * SHARE, SHARE), SHARE), :], panel),
            (cent, full),
        ))
    ]
    for load in loads:
        load.start()

    barrier = pltpu.get_barrier_semaphore()
    up = (lax.rem(z + 1, NZ) * NG + g, q)
    down = (lax.rem(z + NZ - 1, NZ) * NG + g, q)
    for peer in (up, down, (r, right), (r, left), (r, opp)):
        pl.semaphore_signal(barrier, inc=1, device_id=peer, device_id_type=MESH)

    @pl.loop(1, NG)
    def _(i):
        mate = z * NG + lax.rem(g + i, NG)
        pl.semaphore_signal(barrier, inc=1, device_id=(mate, q), device_id_type=MESH)

    for load in loads[:4]:
        load.wait()

    lane = iota((NR, NR), 1)
    row_i = iota((NR, NR), 0)
    count_col = jnp.sum(jnp.where(lane == row_i, counting[...].astype(F32), 0.0), axis=1, keepdims=True)
    par_row = lax.rem(parent[...], PAR).astype(F32)
    listed = []
    for j in range(2):
        wide = jnp.where(lane == row_i, listing[j : j + 1, :].astype(F32), 0.0)
        listed.append(jnp.sum(wide, axis=1, keepdims=True).astype(jnp.int32))
    meta = jnp.zeros((NR, NR), F32)
    for j in range(2):
        hot = (lane == listed[j]) & (count_col > j)
        code = jnp.sum(jnp.where(hot, par_row + 1.0, 0.0), axis=1, keepdims=True)
        meta = meta + jnp.where(lax.rem(lane, 16) == g * 2 + j, code, 0.0)
        picked = jnp.dot(hot.astype(BF16), emb[...], preferred_element_type=F32)
        for k in range(8):
            stage[pl.ds(j * 8 + k, NR, stride=16), :] = picked[:, 128 * k : 128 * (k + 1)]
    tiles[...] = stage[...].astype(BF16)
    meta_o[...] = meta

    pl.semaphore_wait(barrier, 2 + NQ - 1 + NG - 1)

    pl.semaphore_signal(up_sem, inc=1, device_id=down, device_id_type=MESH)
    pl.semaphore_signal(down_sem, inc=1, device_id=up, device_id_type=MESH)

    def send_rows(s, i):
        zt = lax.rem(z + sdz(s), NZ)
        o = zt * NG + lax.rem(g + i, NG)
        remote(
            tiles.at[pl.ds(mult(o * 16, 16), 16)],
            xg.at[pl.ds(mult((s * NQ + q) * 128 + g * 16, 16), 16)],
            zss, zrs.at[s], (o, q),
        ).start()

    @pl.loop(1, NG)
    def _(i):
        send_rows(0, i)

    xg[pl.ds(mult(q * 128 + g * 16, 16), 16), :] = tiles[pl.ds(mult(r * 16, 16), 16), :]
    zb[0:8, :] = meta_o[pl.ds(mult(z * 8, 8), 8), :]

    def chunk(t, qq):
        return xg.at[pl.ds(mult((t * NQ + qq) * 128, 128), 128)]

    def step(s):
        @pl.when(s < NZ)
        def _():
            @pl.when(s > 0)
            def _():
                remote(chunk(s, q), chunk(s, q), zss, zrs.at[s], (r, right)).wait_recv()

            @pl.when(s == 0)
            def _():
                part = xg.at[pl.ds(0, 112)]
                remote(part, part, zss, zrs.at[s], (r, right)).wait_recv()

            for rs, peer in ((xrl, right), (xrr, left), (xrf, opp)):
                remote(chunk(s, q), chunk(s, q), xss, rs.at[s], (r, peer)).start()

        @pl.when(s >= LAG)
        def _():
            t = s - LAG
            for rs, peer in ((xrl, left), (xrr, right), (xrf, opp)):
                remote(chunk(t, q), chunk(t, peer), xss, rs.at[t], (r, peer)).wait_recv()
            rows_f[...] = xg[pl.ds(mult(t * 512, 512), 512), :].astype(F32)
            for k in range(8):
                xs[pl.ds(mult(t * 64, 64), 64), 128 * k : 128 * (k + 1)] = rows_f[
                    pl.ds(k, 64, stride=8), :
                ].astype(BF16)

    def send_steps(first, last):
        @pl.loop(first, last)
        def _(s):
            for i in range(NG):
                send_rows(s, i)

            @pl.when(s >= LEAD)
            def _():
                step(s - LEAD)

    def send_parents(s):
        zt = lax.rem(z + sdz(s), NZ)
        remote(
            meta_o.at[pl.ds(mult(zt * NG, 8), 8)], zb.at[pl.ds(mult(s * 8, 8), 8)],
            mss, mzr, (zt * NG + g, q),
        ).start()

    @pl.loop(1, HALF)
    def _(d):
        pl.semaphore_wait(up_sem, 1)
        pl.semaphore_signal(up_sem, inc=1, device_id=down, device_id_type=MESH)
        pl.semaphore_wait(down_sem, 1)

        @pl.when(d < HALF - 1)
        def _():
            pl.semaphore_signal(down_sem, inc=1, device_id=up, device_id_type=MESH)

        send_parents(2 * d - 1)
        send_parents(2 * d)

        for i in range(NG):
            send_rows(d, i)

    pl.semaphore_wait(up_sem, 1)
    send_parents(NZ - 1)
    send_steps(HALF, NZ)

    for load in loads[4:]:
        load.wait()

    kid = iota((KIDS, 1), 0)
    for p in range(PAR):
        wide = full[p].astype(F32)
        norm = jnp.sum(wide * wide, axis=1, keepdims=True) * TEMP
        norms[p * KIDS : (p + 1) * KIDS, :] = jnp.where(kid < ccount[p], norm, -FLOOR)

    mate = meta_o.at[pl.ds(0, 120)]
    remote(mate, zb.at[pl.ds(0, 120)], mss, mzr, (r, right)).wait_recv()
    for gg in range(NG):
        sb[gg * 16 : (gg + 1) * 16, :] = zb[pl.ds(gg, 16, stride=8), :]

    @pl.loop(1, NG)
    def _(i):
        gt = lax.rem(g + i, NG)
        remote(
            sb.at[pl.ds(mult(gt * 16, 16), 16)], yb.at[pl.ds(mult(g * 16, 16), 16)],
            mss, myr, (z * NG + gt, q),
        ).start()

    yb[pl.ds(mult(g * 16, 16), 16), :] = sb[pl.ds(mult(g * 16, 16), 16), :]

    pl.loop(NZ - LEAD, 10)(step)

    mate = sb.at[pl.ds(0, 112)]
    remote(mate, yb.at[pl.ds(0, 112)], mss, myr, (r, right)).wait_recv()
    slot = yb[0:16, :]
    for gg in range(1, NG):
        slot = slot + yb[gg * 16 : (gg + 1) * 16, :]
    sl = iota((16, 128), 0)
    ln = iota((16, 128), 1)
    mine = lax.rem(lax.div(ln, 16), NQ) == q
    for b in range(8):
        here = mine & (sl == 2 * b + lax.div(ln, 64))
        mx[b : b + 1, :] = jnp.sum(jnp.where(here, slot, 0.0), axis=0, keepdims=True)
    for k, peer in enumerate((right, left, opp)):
        remote(mx, xm.at[pl.ds(mult(q * 8, 8), 8)], mss, mxr, (r, peer)).start()
    xm[pl.ds(mult(q * 8, 8), 8), :] = mx[...]

    pl.loop(10, 12)(step)
    pl.loop(12, NZ)(step)

    mate = xm.at[pl.ds(0, 24)]
    remote(mate, mate, mss, mxr, (r, right)).wait_recv()

    mt[...] = xm[0:8, :] + xm[8:16, :] + xm[16:24, :] + xm[24:32, :]
    wsum[...] = jnp.zeros((COLS, 128), F32)

    def codes(b0, nb):
        return jnp.concatenate([mt[b : b + 1, :] for b in range(b0, b0 + nb)], axis=1)

    def gather_logits(code, kids, lanes):
        logits = jnp.full((kids, lanes), FLOOR, F32)
        for p in range(PAR):
            rows = slice(p * kids, (p + 1) * kids)
            value = lg[rows, 0:lanes] * (2.0 * TEMP) - norms[rows, :]
            logits = jnp.where(code == p + 1.0, value, logits)
        return logits

    def spread(code, b0, nb, share):
        for p in range(PAR):
            rows = slice(p * SHARE, (p + 1) * SHARE)
            value = jnp.where(code == p + 1.0, share, 0.0)
            resp[rows, b0 * 128 : (b0 + nb) * 128] = value.astype(BF16)
            total = value[:, 0:128]
            for b in range(1, nb):
                total = total + value[:, b * 128 : (b + 1) * 128]
            wsum[rows, :] = wsum[rows, :] + total

    def first_pass(b0, nb):
        lanes = nb * 128
        code = codes(b0, nb)
        lg[:, 0:lanes] = lax.dot_general(
            full[...].reshape(PAR * KIDS, D), xs[b0 * 128 : b0 * 128 + lanes, :],
            (((1,), (1,)), ((), ())), preferred_element_type=F32,
        )
        logits = gather_logits(code, KIDS, lanes)
        value = jnp.exp(logits - jnp.max(logits, axis=0, keepdims=True))
        total = jnp.sum(value, axis=0, keepdims=True)
        scale = jnp.where(code > 0.5, 1.0 / total, 0.0)
        terms[...] = value
        spread(code, b0, nb, terms[pl.ds(mult(q * SHARE, SHARE), SHARE), :] * scale)

    def update(last):
        inverse = 1.0 / (jnp.sum(wsum[...], axis=1, keepdims=True) + 1.0)
        square = jnp.zeros((COLS, 1), F32)
        for b in range(4):
            cols = slice(b * 256, (b + 1) * 256)
            sums = jnp.dot(resp[...], xs[:, cols], preferred_element_type=F32)
            old = panel[:, :, cols].reshape(COLS, 256).astype(F32)
            new = (sums + old) * inverse
            if last:
                out[:, :, cols] = new.reshape(PAR, SHARE, 256)
            else:
                low = new.astype(BF16)
                panel[:, :, cols] = low.reshape(PAR, SHARE, 256)
                wide = low.astype(F32)
                square = square + jnp.sum(wide * wide, axis=1, keepdims=True)
        return square

    first_pass(0, 2)
    first_pass(2, 2)
    first_pass(4, 2)
    pl.loop(NZ, NZ + LAG)(step)
    first_pass(6, 2)
    square = update(False)

    kid = iota((SHARE, 1), 0) + q * SHARE
    for p in range(PAR):
        rows = slice(p * SHARE, (p + 1) * SHARE)
        norms[rows, :] = jnp.where(kid < ccount[p], square[rows] * TEMP, -FLOOR)
    wsum[...] = jnp.zeros((COLS, 128), F32)
    for h in range(4):
        code = codes(h * 2, 2)
        lg[0:COLS, 0:256] = lax.dot_general(
            panel[...].reshape(COLS, D), xs[h * 256 : (h + 1) * 256, :],
            (((1,), (1,)), ((), ())), preferred_element_type=F32,
        )
        logits = gather_logits(code, SHARE, 256)
        top = jnp.max(logits, axis=0, keepdims=True)
        value = jnp.exp(logits - top)
        total = jnp.sum(value, axis=0, keepdims=True)
        terms[h * SHARE : (h + 1) * SHARE, :] = value
        for b in range(2):
            sx[h * 2 + b : h * 2 + b + 1, :] = top[:, b * 128 : (b + 1) * 128]
            sx[8 + h * 2 + b : 9 + h * 2 + b, :] = total[:, b * 128 : (b + 1) * 128]
    peers = (right, left, opp)
    for k, peer in enumerate(peers):
        remote(sx, rx.at[pl.ds(k * 16, 16)], sss, srs.at[k], (r, peer)).start()
    tops, totals = [sx[0:8, :]], [sx[8:16, :]]
    for k in range(3):
        remote(sx, rx.at[pl.ds(k * 16, 16)], sss, srs.at[k], (r, right)).wait_recv()
        tops.append(rx[k * 16 : k * 16 + 8, :])
        totals.append(rx[k * 16 + 8 : k * 16 + 16, :])
    top = jnp.maximum(jnp.maximum(tops[0], tops[1]), jnp.maximum(tops[2], tops[3]))
    own = jnp.exp(tops[0] - top)
    total = totals[0] * own
    for k in range(1, 4):
        total = total + totals[k] * jnp.exp(tops[k] - top)
    est[...] = top + jnp.log(total)

    @pl.loop(1, NZ)
    def _(k):
        s = NZ - k
        zt = lax.rem(z + NZ - sdz(s), NZ)
        remote(est, eb.at[z], ess, ezr, (zt * NG + g, q)).start()

    sc[...] = jnp.where(mt[...] > 0.5, own / total, 0.0)
    for h in range(4):
        scale = jnp.concatenate([sc[h * 2 : h * 2 + 1, :], sc[h * 2 + 1 : h * 2 + 2, :]], axis=1)
        spread(codes(h * 2, 2), h * 2, 2, terms[h * SHARE : (h + 1) * SHARE, :] * scale)
    update(True)
    store = pltpu.make_async_copy(out, out_hbm, out_sem)
    store.start()

    def step_of(dz):
        return jnp.where((dz >= 1) & (dz <= HALF), 2 * dz - 1, lax.rem(2 * (NZ - dz), 2 * NZ))

    mate = eb.at[pl.ds(0, NZ - 1)]
    remote(mate, mate, ess, ezr, (r, right)).wait_recv()
    eb[z] = est[...]
    shape = (NZ, 8, 128)
    block = lax.div(step_of(lax.rem(iota(shape, 0) + NZ - z, NZ)), 2)
    fs[...] = jnp.sum(jnp.where(iota(shape, 1) == block, eb[...], 0.0), axis=1)

    @pl.loop(1, NG)
    def _(i):
        gt = lax.rem(g + i, NG)
        remote(fs, fb.at[pl.ds(mult(g * 16, 16), 16)], ess, eyr, (z * NG + gt, q)).start()

    mate = fb.at[pl.ds(0, 112)]
    remote(mate, mate, ess, eyr, (r, right)).wait_recv()
    fb[pl.ds(mult(g * 16, 16), 16), :] = fs[...]
    for gg in range(NG):
        fo[pl.ds(gg, 16, stride=8), :] = fb[gg * 16 : (gg + 1) * 16, :]
    dz = lax.rem(lax.div(row_i, NG) + NZ - z, NZ)
    at = lax.rem(step_of(dz), 2) * 64 + q * 16 + g * 2
    home = jnp.zeros((1, NR), F32)
    for j in range(2):
        hot = (lane == listed[j]) & (count_col > j)
        value = jnp.sum(jnp.where(lane == at + j, fo[...], 0.0), axis=1, keepdims=True)
        home = home + jnp.sum(jnp.where(hot, value, 0.0), axis=0, keepdims=True)
    energy[...] = home

    store.wait()

    def drain(ref, sem):
        remote(ref, ref, sem, eyr, (r, right)).wait_send()

    drain(tiles.at[pl.ds(0, 127 * 16)], zss)
    drain(xg.at[pl.ds(0, 48 * 128)], xss)
    drain(stage.at[pl.ds(0, 256)], mss)
    drain(rx, sss)
    drain(stage.at[pl.ds(0, 232)], ess)


def on_device(embeddings, parent_id, send_list, send_count, child_count, centroids):
    dma = pltpu.SemaphoreType.DMA
    vmem = pl.BlockSpec(memory_space=pltpu.VMEM)
    updated, row_energy = pl.pallas_call(
        kernel,
        name="refine",
        out_shape=(
            jax.ShapeDtypeStruct((PAR, SHARE, D), F32),
            jax.ShapeDtypeStruct((1, NR), F32),
        ),
        in_specs=[pl.BlockSpec(memory_space=pltpu.HBM)] * 6,
        out_specs=(pl.BlockSpec(memory_space=pltpu.HBM), vmem),
        scratch_shapes=[
            pltpu.VMEM((PAR, SHARE, D), F32),
            dma,
            pltpu.VMEM((NR, D), BF16),
            pltpu.VMEM((2, NR), jnp.int32),
            pltpu.VMEM((1, NR), jnp.int32),
            pltpu.VMEM((1, NR), jnp.int32),
            pltpu.SMEM((PAR,), jnp.int32),
            pltpu.VMEM((2048, 128), F32),
            pltpu.VMEM((2048, 128), BF16),
            pltpu.VMEM((64 * 128, 128), BF16),
            pltpu.VMEM((512, 128), F32),
            pltpu.VMEM((1024, D), BF16),
            pltpu.VMEM((PAR, KIDS, D), BF16),
            pltpu.VMEM((PAR, SHARE, D), BF16),
            pltpu.VMEM((PAR * KIDS, 1), F32),
            pltpu.VMEM((PAR * KIDS, 256), F32),
            pltpu.VMEM((KIDS, 256), F32),
            pltpu.VMEM((COLS, 1024), BF16),
            pltpu.VMEM((COLS, 128), F32),
            pltpu.VMEM((128, 128), F32),
            pltpu.VMEM((128, 128), F32),
            pltpu.VMEM((128, 128), F32),
            pltpu.VMEM((128, 128), F32),
            pltpu.VMEM((8, 128), F32),
            pltpu.VMEM((32, 128), F32),
            pltpu.VMEM((8, 128), F32),
            pltpu.VMEM((16, 128), F32),
            pltpu.VMEM((48, 128), F32),
            pltpu.VMEM((8, 128), F32),
            pltpu.VMEM((8, 128), F32),
            pltpu.VMEM((NZ, 8, 128), F32),
            pltpu.VMEM((16, 128), F32),
            pltpu.VMEM((128, 128), F32),
            pltpu.VMEM((128, 128), F32),
            pltpu.SemaphoreType.REGULAR, pltpu.SemaphoreType.REGULAR,
            dma((7,)), dma, dma((NZ,)), dma, dma((NZ,)), dma((NZ,)), dma((NZ,)),
            dma, dma, dma, dma,
            dma, dma((3,)),
            dma, dma, dma,
        ],
        compiler_params=pltpu.CompilerParams(
            collective_id=0, has_side_effects=True, vmem_limit_bytes=60 * 1024 * 1024
        ),
    )(
        embeddings,
        send_list[0].T,
        send_count,
        parent_id[None, :],
        child_count,
        centroids,
    )
    return (updated, row_energy[0])


def solution(mesh):
    in_specs = (
        P(("rows", "rep"), None),
        P(("rows", "rep")),
        P(("rows", "rep"), None, None),
        P(("rows", "rep"), None),
        P("rows"),
        P("rows", None, None),
    )
    out_specs = (P("rows", "rep", None), P(("rows", "rep")))
    return jax.shard_map(
        on_device, mesh=mesh, in_specs=in_specs, out_specs=out_specs, check_vma=False
    )
```
